32 devices in a mesh: row: 8 (over y, x, core), col: 4 (over z).
Axes of the slice: x: 2, y: 2, z: 4, core: 2. Of those that a mesh axis runs over, the one named last changes fastest.
Arguments:
- pool: bfloat16 [4096, 128], P(('row', 'col')), may hold values from -6 to 6
- targets: bfloat16 [4096], P(('row', 'col')), may hold values from -15 to 15
- picks: int32 [512], P(('row', 'col')), may hold values from 0 to 127
- inducing: float32 [8192, 128], replicated, may hold values from -6 to 6
- inv_sq_lengths: float32 [128], replicated, may hold values from 0.04 to 0.12
- prec_old: float32 [8192, 8192], P('row', 'col'), may hold values from -1 to 6, as said below
- mean_old: float32 [8192], P('row'), may hold values from -6 to 6
- panel: int32 [1], replicated, may hold values from 0 to 31
Outputs:
- prec_new: float32 [8192, 8192], P('row', 'col')
- mean_new: float32 [8192], P('row')
The draws below stay inside these ranges and needn't reach their ends.
Inputs may be any that keep to these rules, and one draw needn't show every extreme that they name: `picks`: each entry indexes a row of the dataset block held by the same device as the entry. `prec_old`: symmetric and positive definite.
All inputs are finite; a program needn't handle non-finite values.
Results may differ from the reference program's by a relative error of at most 0.0028.
Values may be sent and summed in bfloat16 or wider, within the bound.
A program may use at most 128 MiB of HBM per device.

```python
import math
import jax
import jax.numpy as jnp
from jax import lax

M = 8192
F = 128
PB = 256
B_DEV = 16
POOL_DEV = 128
B_TOTAL = 512
POOL_TOTAL = 4096


def draw_targets(key, part):
    ramp = jnp.exp(jnp.log(3.0) * jnp.arange(POOL_TOTAL, dtype=jnp.float32) / max(POOL_TOTAL - 1, 1))
    noise = jax.random.normal(key, (POOL_TOTAL,), jnp.float32)
    raw = noise * ramp
    low = jnp.min(raw)
    high = jnp.max(raw)
    scaled = 30.0 * (raw - low) / (high - low) - 15.0
    return jnp.clip(scaled, -15.0, 15.0).astype(jnp.bfloat16)


def draw_prec_old(key, part):
    base_key = jax.random.fold_in(key, 11)
    diag_key = jax.random.fold_in(key, 12)
    base = jax.random.normal(base_key, (M, M), jnp.float32)
    diag_vals = jax.random.uniform(diag_key, (M,), jnp.float32, 3.0, 4.0)
    symmetric = (base + base.T) / jnp.sqrt(2.0 * M)
    symmetric = jnp.clip(symmetric, -0.9, 0.9)
    return symmetric + jnp.diag(diag_vals)


def with_ends(result, rng, least, largest):
    dims = result.shape
    index_at = [jax.random.randint(jax.random.fold_in(rng, axis), (), 0, dims[axis]) for axis in range(len(dims))]
    result = result.at[tuple(index_at)].set(least)
    longest = dims.index(max(dims))
    index_at[longest] = (index_at[longest] + 1) % dims[longest]
    return result.at[tuple(index_at)].set(largest)


def level_of(stream_key, dims, split, smallest, top_value):
    def one(axis_at, blocks):
        draws = jax.random.uniform(jax.random.fold_in(jax.random.fold_in(stream_key, 6), axis_at), (blocks,), jnp.float32, smallest / len(split), top_value / len(split))
        return jnp.repeat(jnp.exp(draws), dims[axis_at] // blocks).reshape((-1,) + (1,) * (len(dims) - axis_at - 1))

    factor_of = one(*split[0])
    for cut in split[1:]:
        factor_of = factor_of * one(*cut)
    return factor_of


def scatter_about(stream_key, shape, deviation, bound, shards=(), held_as=jnp.bfloat16):
    array = deviation * jax.random.normal(stream_key, shape, jnp.float32)
    if shards:
        array = array * level_of(stream_key, shape, shards, -0.22, 0.18)
    return jnp.clip(array, -bound, bound).astype(held_as)


def setup_inputs(seed: int = 0) -> dict:
    streams_of = jax.random.split(jax.random.key(seed), 9)
    return {
        "pool": scatter_about(streams_of[0], (POOL_TOTAL, F), 1.0, 6.0, ((0, 32),)),
        "targets": draw_targets(jax.random.fold_in(streams_of[8], 71), 0),
        "picks": with_ends(jax.random.randint(streams_of[2], (B_TOTAL,), 0, POOL_DEV), jax.random.fold_in(streams_of[2], 1), 0, POOL_DEV - 1).astype(jnp.int32),
        "inducing": scatter_about(streams_of[3], (M, F), 1.0, 6.0, (), jnp.float32),
        "inv_sq_lengths": jnp.clip(jnp.exp(jax.random.uniform(streams_of[4], (F,), jnp.float32, math.log(0.04), math.log(0.12))), 0.04, 0.12),
        "prec_old": draw_prec_old(jax.random.fold_in(streams_of[8], 71), 0),
        "mean_old": scatter_about(streams_of[6], (M,), 1.0, 6.0, ((0, 8),), jnp.float32),
        "panel": jax.random.randint(streams_of[7], (1,), 0, M // PB).astype(jnp.int32),
    }


RATE = 0.5
EPSILON = 1e-05

def kernel_block(points, weights, sample_x):
    sample_f = sample_x.astype(jnp.float32)
    point_sq = lax.optimization_barrier(jnp.sum(points * points * weights, axis=1))
    sample_sq = lax.optimization_barrier(jnp.sum(sample_f * sample_f * weights, axis=1))
    cross_term = lax.dot_general(points * weights, sample_f, (((1,), (1,)), ((), ())), precision=lax.Precision.HIGHEST)
    return jnp.exp(-0.5 * (point_sq[:, None] + sample_sq[None, :] - 2.0 * cross_term)).astype(jnp.bfloat16)

def reference(pool, targets, picks, inducing, inv_sq_lengths, prec_old, mean_old, panel):
    owner_dev = jnp.arange(B_TOTAL, dtype=jnp.int32) // B_DEV
    pool_rows = (owner_dev * POOL_DEV + picks).astype(jnp.int32)
    sample_x = pool[pool_rows]
    sample_y = targets[pool_rows].astype(jnp.float32)
    features = kernel_block(inducing, inv_sq_lengths, sample_x).astype(jnp.float32)
    gram_full = jnp.dot(features, features.T, precision=lax.Precision.HIGHEST)
    fit_full = jnp.dot(features, sample_y, precision=lax.Precision.HIGHEST)
    power_sum = jnp.sum(sample_y * sample_y)
    trace_scale = jnp.trace(gram_full) / M
    joined = (1.0 - RATE) * prec_old + RATE * gram_full / trace_scale
    mean_mid = (1.0 - RATE) * mean_old + RATE * fit_full / jnp.sqrt(trace_scale * (power_sum / B_TOTAL + EPSILON))
    panel_start = (panel[0] * PB).astype(jnp.int32)
    zero_index = jnp.zeros((), jnp.int32)
    diag_block = lax.dynamic_slice(joined, (panel_start, panel_start), (PB, PB))
    factor = jnp.linalg.cholesky(diag_block)
    column_panel = lax.dynamic_slice(joined, (zero_index, panel_start), (M, PB))
    wide_rows = lax.linalg.triangular_solve(factor, column_panel, left_side=False, lower=True, transpose_a=True)
    mean_part = lax.dynamic_slice(mean_mid, (panel_start,), (PB,))
    head_part = lax.linalg.triangular_solve(factor, mean_part[:, None], left_side=True, lower=True)[:, 0]
    updated = joined - jnp.dot(wide_rows, wide_rows.T, precision=lax.Precision.HIGHEST)
    updated = lax.dynamic_update_slice(updated, wide_rows, (zero_index, panel_start))
    updated = lax.dynamic_update_slice(updated, wide_rows.T, (panel_start, zero_index))
    updated = lax.dynamic_update_slice(updated, factor, (panel_start, panel_start))
    mean_next = mean_mid - jnp.dot(wide_rows, head_part, precision=lax.Precision.HIGHEST)
    mean_next = lax.dynamic_update_slice(mean_next, head_part, (panel_start,))
    return (updated, mean_next)
```

```python
import functools

import jax
import jax.numpy as jnp
from jax import lax
from jax.experimental import pallas as pl
from jax.experimental.pallas import tpu as pltpu
from jax.sharding import PartitionSpec as P

PB = 256
RATE = 0.5
EPSILON = 1e-05
SUPER = 64
SUB = 8
LANES = 128
ROWS_STEP = 256
F32 = jnp.float32
BF16 = jnp.bfloat16
HIGHEST = lax.Precision.HIGHEST
NN = (((1,), (0,)), ((), ()))
NT = (((1,), (1,)), ((), ()))
TN = (((0,), (0,)), ((), ()))
MESH = pl.DeviceIdType.MESH


def dot(a, b, dims, precision=None):
    return lax.dot_general(a, b, dims, precision=precision, preferred_element_type=F32)


def split_two(x):
    high = x.astype(BF16)
    return high, (x - high.astype(F32)).astype(BF16)


def dot_split(a, b, dims):
    a_high, a_low = a
    b_high, b_low = b
    return dot(a_high, b_high, dims) + (dot(a_high, b_low, dims) + dot(a_low, b_high, dims))


def prep_kernel(
    info, picks_ref, pool_ref, targets_ref, cols_ref, rows_ref, diag_ref, mean_ref, points_ref,
    xs_out, cols_out, rows_out, diag_out, points_out,
):
    in_row = info[2] == 1
    in_col = info[3] == 1
    pool_count = pool_ref.shape[0]
    batch = picks_ref.shape[1]
    ids = lax.broadcasted_iota(jnp.int32, (pool_count, batch), 0)
    chosen_t = jnp.where(ids == picks_ref[...], 1.0, 0.0).astype(BF16)
    eye = jnp.where(
        lax.broadcasted_iota(jnp.int32, (pool_count, pool_count), 0)
        == lax.broadcasted_iota(jnp.int32, (pool_count, pool_count), 1),
        1.0,
        0.0,
    ).astype(BF16)
    chosen = dot(chosen_t, eye, TN)
    values = jnp.sum(chosen * targets_ref[...].astype(F32), axis=1, keepdims=True)
    samples = dot(chosen_t, pool_ref[...], TN)
    width = samples.shape[1]
    xs_out[:, :width] = samples.astype(BF16)
    xs_out[:, width:] = jnp.broadcast_to(values, (batch, LANES)).astype(BF16)
    zero = jnp.float32(0.0)
    cols_out[...] = jnp.where(in_col, cols_ref[...], zero).astype(BF16)
    rows_out[...] = jnp.where(in_row, rows_ref[...], zero).astype(BF16)
    points_out[...] = points_ref[...]
    both = jnp.logical_and(in_row, in_col)
    diag_out[:PB, :] = jnp.where(both, diag_ref[...], zero)
    diag_out[PB:, :] = jnp.where(
        both, jnp.broadcast_to(mean_ref[...], (diag_out.shape[0] - PB, PB)), zero
    )


def feature_block(points, weights, samples_twice, samples_sq):
    scaled = points * weights
    point_sq = jnp.sum(points * scaled, axis=1, keepdims=True)
    high, low = split_two(scaled)
    cross_term = dot(jnp.concatenate([high, low], axis=1), samples_twice, NT)
    return jnp.exp(cross_term - 0.5 * (point_sq + samples_sq)).astype(BF16)


def eliminate_super(x_ref, base):
    sub_ids = lax.broadcasted_iota(jnp.int32, (SUB, LANES), 0)
    groups = SUPER // SUB
    size = x_ref.shape[0]
    for step in range(groups):
        col0 = base + step * SUB
        lane_tiles = [t for t in range(size // LANES) if (t + 1) * LANES > col0]
        lane_tiles += [size // LANES + t for t in range(size // LANES) if t * LANES < col0 + SUB]
        rows = {
            g: x_ref[base + g * SUB : base + (g + 1) * SUB, col0 : col0 + SUB]
            for g in range(step, groups)
        }
        column = {
            g: [jnp.broadcast_to(rows[g][:, k : k + 1], (SUB, LANES)) for k in range(SUB)]
            for g in rows
        }
        square = {
            (m, k): jnp.broadcast_to(column[step][k][m : m + 1, :], (SUB, LANES))
            for k in range(SUB)
            for m in range(k + 1)
        }
        scale = []
        below = {}
        for k in range(SUB):
            scale.append(lax.rsqrt(square[k, k]))
            for j in range(k + 1, SUB):
                below[j, k] = square[k, j] * scale[k]
            for m in range(k + 1, SUB):
                for j in range(m, SUB):
                    square[m, j] = square[m, j] - below[m, k] * below[j, k]
        factor_cols = {}
        for g in rows:
            for k in range(SUB):
                value = column[g][k]
                for m in range(k):
                    value = value - factor_cols[g, m] * below[k, m]
                factor_cols[g, k] = value * scale[k]
        for t in lane_tiles:
            lanes = slice(t * LANES, (t + 1) * LANES)
            tiles = {
                g: x_ref[base + g * SUB : base + (g + 1) * SUB, lanes] for g in range(step, groups)
            }
            for k in range(SUB):
                pivot_row = jnp.broadcast_to(tiles[step][k : k + 1, :], (SUB, LANES)) * scale[k]
                mine = tiles[step] - jnp.where(sub_ids > k, factor_cols[step, k], 0.0) * pivot_row
                tiles[step] = jnp.where(sub_ids == k, pivot_row, mine)
                for g in range(step + 1, groups):
                    tiles[g] = tiles[g] - factor_cols[g, k] * pivot_row
            for g in tiles:
                x_ref[base + g * SUB : base + (g + 1) * SUB, lanes] = tiles[g]
    after = base + SUPER
    if after < size:
        done = x_ref[base:after, :]
        x_ref[after:, :] = x_ref[after:, :] - dot(done[:, after:size], done, TN, HIGHEST)


def move_kernel(
    n_rows, n_cols,
    points_ref, xs_ref, cols_ref, rows_ref, diag_ref, inducing_ref, weights_ref,
    feat_r_out, feat_c_out, feat_p_out, cols_out, rows_out, x_out, mean_out, stats_out, y_out,
    all_x, diag_got, diag_sum, diag_col, diag_all, cols_got, cols_sum, rows_got, rows_sum, twice,
    send_sem, recv_sem,
):
    my_row = lax.axis_index("row")
    my_col = lax.axis_index("col")
    n_of = {"row": n_rows, "col": n_cols}
    me_of = {"row": my_row, "col": my_col}
    slot = [0]

    def peer(axis, distance):
        return lax.rem(me_of[axis] + distance, n_of[axis])

    def peer_id(axis, distance):
        if axis == "row":
            return (peer(axis, distance), my_col)
        return (my_row, peer(axis, distance))

    def send_all(axis, source, target):
        copies = []
        for distance in range(1, n_of[axis]):
            copy = pltpu.make_async_remote_copy(
                src_ref=source(distance),
                dst_ref=target(distance),
                send_sem=send_sem.at[slot[0]],
                recv_sem=recv_sem.at[slot[0]],
                device_id=peer_id(axis, distance),
                device_id_type=MESH,
            )
            slot[0] += 1
            copy.start()
            copies.append(copy)
        return copies

    def arrive(copies):
        for copy in copies:
            copy.wait_recv()

    started = []

    barrier = pltpu.get_barrier_semaphore()
    for axis in ("row", "col"):
        for distance in range(1, n_of[axis]):
            pl.semaphore_signal(
                barrier, inc=1, device_id=peer_id(axis, distance), device_id_type=MESH
            )
    pl.semaphore_wait(barrier, n_rows + n_cols - 2)

    batch = xs_ref.shape[0]
    all_x[my_col, my_row] = xs_ref[...]
    xs_first = send_all("row", lambda d: xs_ref, lambda d: all_x.at[my_col, my_row])

    def slices(count, ref, axis):
        return lambda d: ref.at[pl.ds(peer(axis, d) * count, count)]

    diag_count = diag_sum.shape[0]
    diag_first = send_all(
        "row", slices(diag_count, diag_ref, "row"), lambda d: diag_got.at[d - 1]
    )
    arrive(xs_first)
    xs_second = send_all("col", lambda d: all_x.at[my_col], lambda d: all_x.at[my_col])

    def combine(ref, got, axis, count):
        total = ref[pl.ds(me_of[axis] * count, count), :]
        for distance in range(1, n_of[axis]):
            total = total + got[distance - 1]
        return total

    arrive(diag_first)
    diag_sum[...] = combine(diag_ref, diag_got, "row", diag_count)
    diag_second = send_all("col", lambda d: diag_sum, lambda d: diag_col.at[d - 1])
    rows_count = rows_sum.shape[0]
    rows_first = send_all(
        "row", slices(rows_count, rows_ref, "row"), lambda d: rows_got.at[d - 1]
    )
    cols_count = cols_sum.shape[0]
    arrive(diag_second)
    total = diag_sum[...]
    for distance in range(1, n_cols):
        total = total + diag_col[distance - 1]
    diag_mine = pl.ds(my_row * diag_count, diag_count)
    diag_all[diag_mine, :] = total
    diag_third = send_all("row", lambda d: diag_all.at[diag_mine], lambda d: diag_all.at[diag_mine])
    arrive(xs_second)
    cols_first = send_all(
        "col", slices(cols_count, cols_ref, "col"), lambda d: cols_got.at[d - 1]
    )

    width = inducing_ref.shape[1]
    n_batch = n_rows * n_cols * batch
    gathered = all_x[...].reshape(n_batch, all_x.shape[3])
    samples = gathered[:, :width]
    twice[:, :width] = samples
    twice[:, width:] = samples
    values_t = jnp.transpose(gathered[:, width:].astype(F32))[:SUB, :]
    y_out[...] = values_t.astype(BF16)
    power = jnp.sum(values_t[:1, :] * values_t[:1, :], keepdims=True)
    weights = weights_ref[...]
    samples_f = samples.astype(F32)
    samples_sq = dot(jnp.broadcast_to(weights, (SUB, width)), samples_f * samples_f, NT, HIGHEST)[:1, :]

    tile_rows = feat_r_out.shape[0]
    tile_cols = feat_c_out.shape[0]
    points_count = inducing_ref.shape[0]

    def features_of(points):
        return feature_block(points, weights, twice[...], samples_sq)

    def trace_step(index, total):
        start = pl.multiple_of(index * PB, PB)
        block = features_of(inducing_ref[pl.ds(start, PB), :])

        @pl.when(start // tile_rows == my_row)
        def _():
            feat_r_out[pl.ds(pl.multiple_of(lax.rem(start, tile_rows), PB), PB), :] = block

        @pl.when(start // tile_cols == my_col)
        def _():
            feat_c_out[pl.ds(pl.multiple_of(lax.rem(start, tile_cols), PB), PB), :] = block

        wide = block.astype(F32)
        return total + jnp.sum((wide * wide).reshape(PB // SUB, SUB, n_batch), axis=0)

    partial = lax.fori_loop(
        0, points_count // PB, trace_step, jnp.zeros((SUB, n_batch), F32)
    )
    trace_scale = jnp.sum(partial, keepdims=True) / points_count
    gram_scale = RATE / trace_scale
    mean_scale = RATE * lax.rsqrt(trace_scale * (power / n_batch + EPSILON))
    stats_out[0:1, :] = jnp.broadcast_to(gram_scale, (1, LANES))
    stats_out[1:2, :] = jnp.broadcast_to(mean_scale, (1, LANES))
    stats_out[2:, :] = jnp.zeros((SUB - 2, LANES), F32)

    arrive(rows_first)
    rows_sum[...] = combine(rows_ref, rows_got, "row", rows_count)
    rows_mine = pl.ds(my_row * rows_count, rows_count)
    rows_out[rows_mine, :] = rows_sum[...]
    rows_second = send_all("row", lambda d: rows_sum, lambda d: rows_out.at[rows_mine])

    feat_p = features_of(points_ref[...])
    feat_p_out[...] = feat_p
    gram_p = dot(feat_p, feat_p, NT)
    arrive(diag_third)
    mean_out[...] = diag_all[PB : PB + SUB, :]
    x_out[:, :PB] = (1.0 - RATE) * diag_all[:PB, :] + gram_scale * gram_p
    x_out[:, PB:] = jnp.where(
        lax.broadcasted_iota(jnp.int32, (PB, PB), 0) == lax.broadcasted_iota(jnp.int32, (PB, PB), 1),
        1.0,
        0.0,
    )
    for base in range(0, PB, SUPER):
        eliminate_super(x_out, base)
        if base == 0:
            arrive(cols_first)
            cols_sum[...] = combine(cols_ref, cols_got, "col", cols_count)
            cols_mine = pl.ds(my_col * cols_count, cols_count)
            cols_out[cols_mine, :] = cols_sum[...]
            cols_second = send_all("col", lambda d: cols_sum, lambda d: cols_out.at[cols_mine])
    arrive(rows_second)
    arrive(cols_second)
    for copies in (
        xs_first, xs_second, diag_first, diag_second, diag_third,
        rows_first, rows_second, cols_first, cols_second,
    ):
        for copy in copies:
            copy.wait_send()


def tile_kernel(
    info,
    prec_ref, feat_r_ref, feat_c_ref, feat_p_ref, cols_ref, rows_ref, x_ref, mean_p_ref,
    stats_ref, y_ref, mean_ref,
    out_ref, mean_out,
    solved, solved_high, solved_low, inverse_high, inverse_low, head,
):
    step = pl.program_id(0)
    in_row = info[2] == 1
    in_col = info[3] == 1
    keep = 1.0 - RATE
    gram_scale = stats_ref[0:1, 0:1]
    mean_scale = stats_ref[1:2, 0:1]

    @pl.when(step == 0)
    def _():
        inverse = x_ref[:, PB:]
        high, low = split_two(inverse)
        inverse_high[...] = high
        inverse_low[...] = low
        joined = keep * rows_ref[...].astype(F32) + gram_scale * dot(feat_p_ref[...], feat_c_ref[...], NT)
        result = dot_split((high, low), split_two(joined), NN)
        solved[...] = result
        solved_high[...], solved_low[...] = split_two(result)
        fit = dot(y_ref[...], feat_p_ref[...], NT)
        head[...] = dot(keep * mean_p_ref[...] + mean_scale * fit, inverse, NT, HIGHEST)

    feat_r = feat_r_ref[...]
    piece = keep * cols_ref[...].astype(F32) + gram_scale * dot(feat_r, feat_p_ref[...], NT)
    wide = dot_split(split_two(piece), (inverse_high[...], inverse_low[...]), NT)
    wide_high, wide_low = split_two(wide)
    tile = keep * prec_ref[...] + gram_scale * dot(feat_r, feat_c_ref[...], NT)
    out_ref[...] = tile - dot_split(
        (wide_high, wide_low), (solved_high[...], solved_low[...]), NN
    )
    fit = dot(y_ref[...], feat_r, NT)
    mean_next = (
        keep * mean_ref[...] + mean_scale * fit[:1, :] - dot(head[...], wide, NT, HIGHEST)[:1, :]
    )
    mean_out[...] = mean_next
    col0 = pl.multiple_of(info[1] * PB, PB)

    @pl.when(in_col)
    def _():
        out_ref[:, pl.ds(col0, PB)] = wide

    here = jnp.logical_and(in_row, step == info[0])

    @pl.when(here)
    def _():
        out_ref[...] = solved[...]
        mean_out[...] = head[:1, :]

    @pl.when(jnp.logical_and(here, in_col))
    def _():
        factor = jnp.transpose(x_ref[:, :PB])
        lower = lax.broadcasted_iota(jnp.int32, (PB, PB), 0) >= lax.broadcasted_iota(
            jnp.int32, (PB, PB), 1
        )
        out_ref[:, pl.ds(col0, PB)] = jnp.where(lower, factor, 0.0)


def whole(memory=pltpu.VMEM):
    return pl.BlockSpec(memory_space=memory)


def local(pool, targets, picks, inducing, inv_sq_lengths, prec_old, mean_old, panel):
    n_rows = lax.axis_size("row")
    n_cols = lax.axis_size("col")
    my_row = lax.axis_index("row")
    my_col = lax.axis_index("col")
    tile_rows, tile_cols = prec_old.shape
    batch = picks.shape[0]
    n_batch = batch * n_rows * n_cols
    width = pool.shape[1]
    row_blocks = tile_rows // PB
    col_blocks = tile_cols // PB
    index = panel[0]
    info = jnp.stack(
        [
            lax.rem(index, row_blocks),
            lax.rem(index, col_blocks),
            (index // row_blocks == my_row).astype(jnp.int32),
            (index // col_blocks == my_col).astype(jnp.int32),
            index,
        ]
    )
    mean_row = mean_old.reshape(1, tile_rows)
    shape = jax.ShapeDtypeStruct
    diag_count = -(-(PB + SUB) // (n_rows * SUB)) * SUB
    diag_rows = diag_count * n_rows
    full = lambda *dims: pl.BlockSpec(dims, lambda i, info: (0,) * len(dims))
    xs, cols, rows, diag, points = pl.pallas_call(
        prep_kernel,
        grid_spec=pltpu.PrefetchScalarGridSpec(
            num_scalar_prefetch=1,
            grid=(1,),
            in_specs=[
                full(1, batch),
                full(*pool.shape),
                full(1, pool.shape[0]),
                pl.BlockSpec((tile_rows, PB), lambda i, info: (0, info[1])),
                pl.BlockSpec((PB, tile_cols), lambda i, info: (info[0], 0)),
                pl.BlockSpec((PB, PB), lambda i, info: (info[0], info[1])),
                pl.BlockSpec((1, PB), lambda i, info: (0, info[0])),
                pl.BlockSpec((PB, width), lambda i, info: (info[4], 0)),
            ],
            out_specs=[
                full(batch, width + LANES),
                full(tile_rows, PB),
                full(PB, tile_cols),
                full(diag_rows, PB),
                full(PB, width),
            ],
        ),
        out_shape=[
            shape((batch, width + LANES), BF16),
            shape((tile_rows, PB), BF16),
            shape((PB, tile_cols), BF16),
            shape((diag_rows, PB), F32),
            shape((PB, width), F32),
        ],
        compiler_params=pltpu.CompilerParams(vmem_limit_bytes=40 << 20),
        name="prep",
    )(
        info, picks.reshape(1, batch), pool, targets.reshape(1, -1),
        prec_old, prec_old, prec_old, mean_row, inducing,
    )
    sems = 5 * (n_rows - 1) + 4 * (n_cols - 1)
    cols_count = tile_rows // n_cols
    rows_count = PB // n_rows
    moved = pl.pallas_call(
        functools.partial(move_kernel, n_rows, n_cols),
        in_specs=[whole()] * 7,
        out_specs=[whole()] * 9,
        out_shape=[
            shape((tile_rows, n_batch), BF16),
            shape((tile_cols, n_batch), BF16),
            shape((PB, n_batch), BF16),
            shape((tile_rows, PB), BF16),
            shape((PB, tile_cols), BF16),
            shape((PB, 2 * PB), F32),
            shape((SUB, PB), F32),
            shape((SUB, LANES), F32),
            shape((SUB, n_batch), BF16),
        ],
        scratch_shapes=[
            pltpu.VMEM((n_cols, n_rows, batch, width + LANES), BF16),
            pltpu.VMEM((n_rows - 1, diag_count, PB), F32),
            pltpu.VMEM((diag_count, PB), F32),
            pltpu.VMEM((n_cols - 1, diag_count, PB), F32),
            pltpu.VMEM((diag_rows, PB), F32),
            pltpu.VMEM((n_cols - 1, cols_count, PB), BF16),
            pltpu.VMEM((cols_count, PB), BF16),
            pltpu.VMEM((n_rows - 1, rows_count, tile_cols), BF16),
            pltpu.VMEM((rows_count, tile_cols), BF16),
            pltpu.VMEM((n_batch, 2 * width), BF16),
            pltpu.SemaphoreType.DMA((sems,)),
            pltpu.SemaphoreType.DMA((sems,)),
        ],
        compiler_params=pltpu.CompilerParams(
            collective_id=0, has_side_effects=True, vmem_limit_bytes=56 << 20
        ),
        name="move",
    )(points, xs, cols, rows, diag, inducing, inv_sq_lengths.reshape(1, width))
    feat_r, feat_c, feat_p, got_cols, got_rows, x, mean_p, stats, y = moved
    step_rows = PB
    updated, mean_next = pl.pallas_call(
        tile_kernel,
        grid_spec=pltpu.PrefetchScalarGridSpec(
            num_scalar_prefetch=1,
            grid=(tile_rows // step_rows,),
            in_specs=[
                pl.BlockSpec((step_rows, tile_cols), lambda i, info: (i, 0)),
                pl.BlockSpec((step_rows, n_batch), lambda i, info: (i, 0)),
                full(tile_cols, n_batch),
                full(PB, n_batch),
                pl.BlockSpec((step_rows, PB), lambda i, info: (i, 0)),
                full(PB, tile_cols),
                full(PB, 2 * PB),
                full(SUB, PB),
                full(SUB, LANES),
                full(SUB, n_batch),
                pl.BlockSpec((1, step_rows), lambda i, info: (0, i)),
            ],
            out_specs=[
                pl.BlockSpec((step_rows, tile_cols), lambda i, info: (i, 0)),
                pl.BlockSpec((1, step_rows), lambda i, info: (0, i)),
            ],
            scratch_shapes=[
                pltpu.VMEM((PB, tile_cols), F32),
                pltpu.VMEM((PB, tile_cols), BF16),
                pltpu.VMEM((PB, tile_cols), BF16),
                pltpu.VMEM((PB, PB), BF16),
                pltpu.VMEM((PB, PB), BF16),
                pltpu.VMEM((SUB, PB), F32),
            ],
        ),
        out_shape=[shape((tile_rows, tile_cols), F32), shape((1, tile_rows), F32)],
        compiler_params=pltpu.CompilerParams(vmem_limit_bytes=56 << 20),
        name="tile",
    )(
        info, prec_old, feat_r, feat_c, feat_p, got_cols, got_rows, x, mean_p, stats, y, mean_row,
    )
    return updated, mean_next.reshape(tile_rows)


def solution(mesh):
    in_specs = (
        P(("row", "col"), None),
        P(("row", "col")),
        P(("row", "col")),
        P(),
        P(),
        P("row", "col"),
        P("row"),
        P(),
    )
    out_specs = (P("row", "col"), P("row"))
    return jax.shard_map(local, mesh=mesh, in_specs=in_specs, out_specs=out_specs, check_vma=False)
```

```python
import functools

import jax
import jax.numpy as jnp
from jax import lax
from jax.experimental import pallas as pl
from jax.experimental.pallas import tpu as pltpu
from jax.sharding import PartitionSpec as P

PB = 256
RATE = 0.5
EPSILON = 1e-05
SUPER = 64
SUB = 8
LANES = 128
VMEM = 62 << 20
F32 = jnp.float32
BF16 = jnp.bfloat16
HIGHEST = lax.Precision.HIGHEST
NN = (((1,), (0,)), ((), ()))
NT = (((1,), (1,)), ((), ()))
TN = (((0,), (0,)), ((), ()))
MESH = pl.DeviceIdType.MESH


def dot(a, b, dims, precision=None):
    return lax.dot_general(a, b, dims, precision=precision, preferred_element_type=F32)


def split_two(x):
    high = x.astype(BF16)
    return high, (x - high.astype(F32)).astype(BF16)


def dot_split(a, b, dims):
    a_high, a_low = a
    b_high, b_low = b
    return dot(a_high, b_high, dims) + (dot(a_high, b_low, dims) + dot(a_low, b_high, dims))


def prep_kernel(
    info, picks_ref, pool_ref, targets_ref, cols_ref, rows_ref, diag_ref, mean_ref, points_ref,
    xs_out, cols_out, rows_out, diag_out, points_out,
):
    in_row = info[2] == 1
    in_col = info[3] == 1
    pool_count = pool_ref.shape[0]
    batch = picks_ref.shape[1]
    ids = lax.broadcasted_iota(jnp.int32, (pool_count, batch), 0)
    chosen_t = jnp.where(ids == picks_ref[...], 1.0, 0.0).astype(BF16)
    eye = jnp.where(
        lax.broadcasted_iota(jnp.int32, (pool_count, pool_count), 0)
        == lax.broadcasted_iota(jnp.int32, (pool_count, pool_count), 1),
        1.0,
        0.0,
    ).astype(BF16)
    chosen = dot(chosen_t, eye, TN)
    values = jnp.sum(chosen * targets_ref[...].astype(F32), axis=1, keepdims=True)
    samples = dot(chosen_t, pool_ref[...], TN)
    width = samples.shape[1]
    xs_out[:, :width] = samples.astype(BF16)
    xs_out[:, width:] = jnp.broadcast_to(values, (batch, LANES)).astype(BF16)
    zero = jnp.float32(0.0)
    cols_out[...] = jnp.where(in_col, cols_ref[...], zero).astype(BF16)
    rows_out[...] = jnp.where(in_row, rows_ref[...], zero).astype(BF16)
    points_out[...] = points_ref[...]
    both = jnp.logical_and(in_row, in_col)
    diag_out[:PB, :] = jnp.where(both, diag_ref[...], zero)
    diag_out[PB:, :] = jnp.where(
        both, jnp.broadcast_to(mean_ref[...], (diag_out.shape[0] - PB, PB)), zero
    )


def feature_block(points, weights, samples_twice, samples_sq):
    scaled = points * weights
    point_sq = jnp.sum(points * scaled, axis=1, keepdims=True)
    high, low = split_two(scaled)
    cross_term = dot(jnp.concatenate([high, low], axis=1), samples_twice, NT)
    return jnp.exp(cross_term - 0.5 * (point_sq + samples_sq))


def eliminate_super(x_ref, base):
    sub_ids = lax.broadcasted_iota(jnp.int32, (SUB, LANES), 0)
    groups = SUPER // SUB
    size = x_ref.shape[0]
    for step in range(groups):
        col0 = base + step * SUB
        lane_tiles = [t for t in range(size // LANES) if (t + 1) * LANES > col0]
        lane_tiles += [size // LANES + t for t in range(size // LANES) if t * LANES < col0 + SUB]
        rows = {
            g: x_ref[base + g * SUB : base + (g + 1) * SUB, col0 : col0 + SUB]
            for g in range(step, groups)
        }
        column = {
            g: [jnp.broadcast_to(rows[g][:, k : k + 1], (SUB, LANES)) for k in range(SUB)]
            for g in rows
        }
        square = {
            (m, k): jnp.broadcast_to(column[step][k][m : m + 1, :], (SUB, LANES))
            for k in range(SUB)
            for m in range(k + 1)
        }
        scale = []
        below = {}
        for k in range(SUB):
            scale.append(lax.rsqrt(square[k, k]))
            for j in range(k + 1, SUB):
                below[j, k] = square[k, j] * scale[k]
            for m in range(k + 1, SUB):
                for j in range(m, SUB):
                    square[m, j] = square[m, j] - below[m, k] * below[j, k]
        factor_cols = {}
        for g in rows:
            for k in range(SUB):
                value = column[g][k]
                for m in range(k):
                    value = value - factor_cols[g, m] * below[k, m]
                factor_cols[g, k] = value * scale[k]
        for t in lane_tiles:
            lanes = slice(t * LANES, (t + 1) * LANES)
            tiles = {
                g: x_ref[base + g * SUB : base + (g + 1) * SUB, lanes] for g in range(step, groups)
            }
            for k in range(SUB):
                pivot_row = jnp.broadcast_to(tiles[step][k : k + 1, :], (SUB, LANES)) * scale[k]
                mine = tiles[step] - jnp.where(sub_ids > k, factor_cols[step, k], 0.0) * pivot_row
                tiles[step] = jnp.where(sub_ids == k, pivot_row, mine)
                for g in range(step + 1, groups):
                    tiles[g] = tiles[g] - factor_cols[g, k] * pivot_row
            for g in tiles:
                x_ref[base + g * SUB : base + (g + 1) * SUB, lanes] = tiles[g]
    after = base + SUPER
    if after < size:
        done = x_ref[base:after, :]
        x_ref[after:, :] = x_ref[after:, :] - dot(done[:, after:size], done, TN, HIGHEST)


def move_kernel(
    n_rows, n_cols,
    points_ref, xs_ref, cols_ref, rows_ref, diag_ref, inducing_ref, weights_ref,
    feat_r_out, feat_c_out, feat_p_out, cols_out, rows_out, x_out, mean_out, stats_out, y_out,
    points_v, feat_r, feat_c,
    all_x, diag_got, diag_sum, diag_col, diag_all, cols_got, cols_sum, rows_got, rows_sum, twice,
    send_sem, recv_sem, local_sem,
):
    my_row = lax.axis_index("row")
    my_col = lax.axis_index("col")
    n_of = {"row": n_rows, "col": n_cols}
    me_of = {"row": my_row, "col": my_col}
    slot = [0]

    def peer(axis, distance):
        return lax.rem(me_of[axis] + distance, n_of[axis])

    def peer_id(axis, distance):
        if axis == "row":
            return (peer(axis, distance), my_col)
        return (my_row, peer(axis, distance))

    def send_all(axis, source, target):
        copies = []
        for distance in range(1, n_of[axis]):
            copy = pltpu.make_async_remote_copy(
                src_ref=source(distance),
                dst_ref=target(distance),
                send_sem=send_sem.at[slot[0]],
                recv_sem=recv_sem.at[slot[0]],
                device_id=peer_id(axis, distance),
                device_id_type=MESH,
            )
            slot[0] += 1
            copy.start()
            copies.append(copy)
        return copies

    def arrive(copies):
        for copy in copies:
            copy.wait_recv()

    load_points = pltpu.make_async_copy(inducing_ref, points_v, local_sem.at[0])
    load_points.start()

    barrier = pltpu.get_barrier_semaphore()
    for axis in ("row", "col"):
        for distance in range(1, n_of[axis]):
            pl.semaphore_signal(
                barrier, inc=1, device_id=peer_id(axis, distance), device_id_type=MESH
            )
    pl.semaphore_wait(barrier, n_rows + n_cols - 2)

    batch = xs_ref.shape[0]
    all_x[my_col, my_row] = xs_ref[...]
    xs_first = send_all("row", lambda d: xs_ref, lambda d: all_x.at[my_col, my_row])

    def slices(count, ref, axis):
        return lambda d: ref.at[pl.ds(peer(axis, d) * count, count)]

    def combine(ref, got, axis, count):
        total = ref[pl.ds(me_of[axis] * count, count), :]
        for distance in range(1, n_of[axis]):
            total = total + got[distance - 1]
        return total

    diag_count = diag_sum.shape[0]
    rows_count = rows_sum.shape[0]
    cols_count = cols_sum.shape[0]
    diag_mine = pl.ds(my_row * diag_count, diag_count)
    rows_mine = pl.ds(my_row * rows_count, rows_count)
    cols_mine = pl.ds(my_col * cols_count, cols_count)
    diag_first = send_all(
        "row", slices(diag_count, diag_ref, "row"), lambda d: diag_got.at[d - 1]
    )
    arrive(xs_first)
    xs_second = send_all("col", lambda d: all_x.at[my_col], lambda d: all_x.at[my_col])
    cols_first = send_all(
        "col", slices(cols_count, cols_ref, "col"), lambda d: cols_got.at[d - 1]
    )
    arrive(diag_first)
    diag_sum[...] = combine(diag_ref, diag_got, "row", diag_count)
    diag_second = send_all("col", lambda d: diag_sum, lambda d: diag_col.at[d - 1])
    rows_first = send_all(
        "row", slices(rows_count, rows_ref, "row"), lambda d: rows_got.at[d - 1]
    )
    arrive(xs_second)

    width = inducing_ref.shape[1]
    n_batch = n_rows * n_cols * batch
    gathered = all_x[...].reshape(n_batch, all_x.shape[3])
    samples = gathered[:, :width]
    twice[:, :width] = samples
    twice[:, width:] = samples
    values_t = jnp.transpose(gathered[:, width:].astype(F32))[:SUB, :]
    y_out[...] = values_t.astype(BF16)
    power = jnp.sum(values_t[:1, :] * values_t[:1, :], keepdims=True)
    weights = weights_ref[...]
    samples_f = samples.astype(F32)
    samples_sq = dot(jnp.broadcast_to(weights, (SUB, width)), samples_f * samples_f, NT, HIGHEST)[:1, :]

    tile_rows = feat_r.shape[0]
    tile_cols = feat_c.shape[0]
    points_count = inducing_ref.shape[0]

    def features_of(points):
        return feature_block(points, weights, twice[...], samples_sq)

    step_rows = min(2 * PB, tile_rows, tile_cols)

    def trace_step(index, total):
        start = pl.multiple_of(index * step_rows, step_rows)
        exact = features_of(points_v[pl.ds(start, step_rows), :])
        block = exact.astype(BF16)

        @pl.when(start // tile_rows == my_row)
        def _():
            feat_r[pl.ds(pl.multiple_of(lax.rem(start, tile_rows), step_rows), step_rows), :] = block

        @pl.when(start // tile_cols == my_col)
        def _():
            feat_c[pl.ds(pl.multiple_of(lax.rem(start, tile_cols), step_rows), step_rows), :] = block

        return total + jnp.sum((exact * exact).reshape(step_rows // SUB, SUB, n_batch), axis=0)

    load_points.wait()
    partial = jnp.zeros((SUB, n_batch), F32)
    quarter = points_count // step_rows // 4
    for part in range(4):
        partial = lax.fori_loop(part * quarter, (part + 1) * quarter, trace_step, partial)
        if part == 1:
            arrive(diag_second)
            total = diag_sum[...]
            for distance in range(1, n_cols):
                total = total + diag_col[distance - 1]
            diag_all[diag_mine, :] = total
            diag_third = send_all(
                "row", lambda d: diag_all.at[diag_mine], lambda d: diag_all.at[diag_mine]
            )
        if part == 2:
            arrive(cols_first)
            cols_sum[...] = combine(cols_ref, cols_got, "col", cols_count)
            cols_out[cols_mine, :] = cols_sum[...]
            cols_second = send_all("col", lambda d: cols_sum, lambda d: cols_out.at[cols_mine])
    stores = [
        pltpu.make_async_copy(feat_r, feat_r_out, local_sem.at[1]),
        pltpu.make_async_copy(feat_c, feat_c_out, local_sem.at[2]),
    ]
    for store in stores:
        store.start()
    trace_scale = jnp.sum(partial, keepdims=True) / points_count
    gram_scale = RATE / trace_scale
    mean_scale = RATE * lax.rsqrt(trace_scale * (power / n_batch + EPSILON))
    stats_out[0:1, :] = jnp.broadcast_to(gram_scale, (1, LANES))
    stats_out[1:2, :] = jnp.broadcast_to(mean_scale, (1, LANES))
    stats_out[2:, :] = jnp.zeros((SUB - 2, LANES), F32)

    arrive(rows_first)
    rows_sum[...] = combine(rows_ref, rows_got, "row", rows_count)
    rows_out[rows_mine, :] = rows_sum[...]
    rows_second = send_all("row", lambda d: rows_sum, lambda d: rows_out.at[rows_mine])

    feat_p = features_of(points_ref[...]).astype(BF16)
    feat_p_out[...] = feat_p
    gram_p = dot(feat_p, feat_p, NT)
    arrive(diag_third)
    mean_out[...] = diag_all[PB : PB + SUB, :]
    x_out[:, :PB] = (1.0 - RATE) * diag_all[:PB, :] + gram_scale * gram_p
    x_out[:, PB:] = jnp.where(
        lax.broadcasted_iota(jnp.int32, (PB, PB), 0) == lax.broadcasted_iota(jnp.int32, (PB, PB), 1),
        1.0,
        0.0,
    )
    for base in range(0, PB, SUPER):
        eliminate_super(x_out, base)
    arrive(rows_second)
    arrive(cols_second)
    for copies in (
        xs_first, xs_second, diag_first, diag_second, diag_third,
        rows_first, rows_second, cols_first, cols_second,
    ):
        for copy in copies:
            copy.wait_send()
    for store in stores:
        store.wait()


def tile_kernel(
    info,
    prec_ref, feat_r_ref, feat_c_ref, feat_p_ref, cols_ref, rows_ref, x_ref, mean_p_ref,
    stats_ref, y_ref, mean_ref,
    out_ref, mean_out,
    solved, solved_parts, inverse_high, inverse_low, head,
):
    step = pl.program_id(0)
    in_row = info[2] == 1
    in_col = info[3] == 1
    keep = 1.0 - RATE
    gram_scale = stats_ref[0:1, 0:1]
    mean_scale = stats_ref[1:2, 0:1]

    @pl.when(step == 0)
    def _():
        inverse = x_ref[:, PB:]
        high, low = split_two(inverse)
        inverse_high[...] = high
        inverse_low[...] = low
        joined = keep * rows_ref[...].astype(F32) + gram_scale * dot(feat_p_ref[...], feat_c_ref[...], NT)
        result = dot_split((high, low), split_two(joined), NN)
        solved[...] = result
        result_high, result_low = split_two(result)
        solved_parts[:PB, :] = result_high
        solved_parts[PB : 2 * PB, :] = result_high
        solved_parts[2 * PB :, :] = result_low
        fit = dot(y_ref[...], feat_p_ref[...], NT)
        head[...] = dot(keep * mean_p_ref[...] + mean_scale * fit, inverse, NT, HIGHEST)

    feat_r = feat_r_ref[...]
    piece = keep * cols_ref[...].astype(F32) + gram_scale * dot(feat_r, feat_p_ref[...], NT)
    wide = dot_split(split_two(piece), (inverse_high[...], inverse_low[...]), NT)
    wide_high, wide_low = split_two(wide)
    tile = keep * prec_ref[...] + gram_scale * dot(feat_r, feat_c_ref[...], NT)
    wide_parts = jnp.concatenate([wide_high, wide_low, wide_high], axis=1)
    out_ref[...] = tile - dot(wide_parts, solved_parts[...], NN)
    fit = dot(y_ref[...], feat_r, NT)
    mean_next = (
        keep * mean_ref[...] + mean_scale * fit[:1, :] - dot_split(split_two(head[...]), (wide_high, wide_low), NT)[:1, :]
    )
    mean_out[...] = mean_next
    col0 = pl.multiple_of(info[1] * PB, PB)

    @pl.when(in_col)
    def _():
        out_ref[:, pl.ds(col0, PB)] = wide

    here = jnp.logical_and(in_row, step == info[0])

    @pl.when(here)
    def _():
        out_ref[...] = solved[...]
        mean_out[...] = head[:1, :]

    @pl.when(jnp.logical_and(here, in_col))
    def _():
        factor = jnp.transpose(x_ref[:, :PB])
        lower = lax.broadcasted_iota(jnp.int32, (PB, PB), 0) >= lax.broadcasted_iota(
            jnp.int32, (PB, PB), 1
        )
        out_ref[:, pl.ds(col0, PB)] = jnp.where(lower, factor, 0.0)


def whole(memory=pltpu.VMEM):
    return pl.BlockSpec(memory_space=memory)


def local(pool, targets, picks, inducing, inv_sq_lengths, prec_old, mean_old, panel):
    n_rows = lax.axis_size("row")
    n_cols = lax.axis_size("col")
    my_row = lax.axis_index("row")
    my_col = lax.axis_index("col")
    tile_rows, tile_cols = prec_old.shape
    batch = picks.shape[0]
    n_batch = batch * n_rows * n_cols
    width = pool.shape[1]
    row_blocks = tile_rows // PB
    col_blocks = tile_cols // PB
    index = panel[0]
    info = jnp.stack(
        [
            lax.rem(index, row_blocks),
            lax.rem(index, col_blocks),
            (index // row_blocks == my_row).astype(jnp.int32),
            (index // col_blocks == my_col).astype(jnp.int32),
            index,
        ]
    )
    mean_row = mean_old.reshape(1, tile_rows)
    shape = jax.ShapeDtypeStruct
    diag_count = -(-(PB + SUB) // (n_rows * SUB)) * SUB
    diag_rows = diag_count * n_rows
    full = lambda *dims: pl.BlockSpec(dims, lambda i, info: (0,) * len(dims))
    xs, cols, rows, diag, points = pl.pallas_call(
        prep_kernel,
        grid_spec=pltpu.PrefetchScalarGridSpec(
            num_scalar_prefetch=1,
            grid=(1,),
            in_specs=[
                full(1, batch),
                full(*pool.shape),
                full(1, pool.shape[0]),
                pl.BlockSpec((tile_rows, PB), lambda i, info: (0, info[1])),
                pl.BlockSpec((PB, tile_cols), lambda i, info: (info[0], 0)),
                pl.BlockSpec((PB, PB), lambda i, info: (info[0], info[1])),
                pl.BlockSpec((1, PB), lambda i, info: (0, info[0])),
                pl.BlockSpec((PB, width), lambda i, info: (info[4], 0)),
            ],
            out_specs=[
                full(batch, width + LANES),
                full(tile_rows, PB),
                full(PB, tile_cols),
                full(diag_rows, PB),
                full(PB, width),
            ],
        ),
        out_shape=[
            shape((batch, width + LANES), BF16),
            shape((tile_rows, PB), BF16),
            shape((PB, tile_cols), BF16),
            shape((diag_rows, PB), F32),
            shape((PB, width), F32),
        ],
        compiler_params=pltpu.CompilerParams(vmem_limit_bytes=VMEM),
        name="prep",
    )(
        info, picks.reshape(1, batch), pool, targets.reshape(1, -1),
        prec_old, prec_old, prec_old, mean_row, inducing,
    )
    sems = 5 * (n_rows - 1) + 4 * (n_cols - 1)
    cols_count = tile_rows // n_cols
    rows_count = PB // n_rows
    moved = pl.pallas_call(
        functools.partial(move_kernel, n_rows, n_cols),
        in_specs=[whole()] * 5 + [whole(pl.ANY), whole()],
        out_specs=[whole(pl.ANY)] * 2 + [whole()] * 7,
        out_shape=[
            shape((tile_rows, n_batch), BF16),
            shape((tile_cols, n_batch), BF16),
            shape((PB, n_batch), BF16),
            shape((tile_rows, PB), BF16),
            shape((PB, tile_cols), BF16),
            shape((PB, 2 * PB), F32),
            shape((SUB, PB), F32),
            shape((SUB, LANES), F32),
            shape((SUB, n_batch), BF16),
        ],
        scratch_shapes=[
            pltpu.VMEM(inducing.shape, F32),
            pltpu.VMEM((tile_rows, n_batch), BF16),
            pltpu.VMEM((tile_cols, n_batch), BF16),
            pltpu.VMEM((n_cols, n_rows, batch, width + LANES), BF16),
            pltpu.VMEM((n_rows - 1, diag_count, PB), F32),
            pltpu.VMEM((diag_count, PB), F32),
            pltpu.VMEM((n_cols - 1, diag_count, PB), F32),
            pltpu.VMEM((diag_rows, PB), F32),
            pltpu.VMEM((n_cols - 1, cols_count, PB), BF16),
            pltpu.VMEM((cols_count, PB), BF16),
            pltpu.VMEM((n_rows - 1, rows_count, tile_cols), BF16),
            pltpu.VMEM((rows_count, tile_cols), BF16),
            pltpu.VMEM((n_batch, 2 * width), BF16),
            pltpu.SemaphoreType.DMA((sems,)),
            pltpu.SemaphoreType.DMA((sems,)),
            pltpu.SemaphoreType.DMA((3,)),
        ],
        compiler_params=pltpu.CompilerParams(
            collective_id=0, has_side_effects=True, vmem_limit_bytes=VMEM
        ),
        name="move",
    )(points, xs, cols, rows, diag, inducing, inv_sq_lengths.reshape(1, width))
    feat_r, feat_c, feat_p, got_cols, got_rows, x, mean_p, stats, y = moved
    step_rows = PB
    updated, mean_next = pl.pallas_call(
        tile_kernel,
        grid_spec=pltpu.PrefetchScalarGridSpec(
            num_scalar_prefetch=1,
            grid=(tile_rows // step_rows,),
            in_specs=[
                pl.BlockSpec((step_rows, tile_cols), lambda i, info: (i, 0)),
                pl.BlockSpec((step_rows, n_batch), lambda i, info: (i, 0)),
                full(tile_cols, n_batch),
                full(PB, n_batch),
                pl.BlockSpec((step_rows, PB), lambda i, info: (i, 0)),
                full(PB, tile_cols),
                full(PB, 2 * PB),
                full(SUB, PB),
                full(SUB, LANES),
                full(SUB, n_batch),
                pl.BlockSpec((1, step_rows), lambda i, info: (0, i)),
            ],
            out_specs=[
                pl.BlockSpec((step_rows, tile_cols), lambda i, info: (i, 0)),
                pl.BlockSpec((1, step_rows), lambda i, info: (0, i)),
            ],
            scratch_shapes=[
                pltpu.VMEM((PB, tile_cols), F32),
                pltpu.VMEM((3 * PB, tile_cols), BF16),
                pltpu.VMEM((PB, PB), BF16),
                pltpu.VMEM((PB, PB), BF16),
                pltpu.VMEM((SUB, PB), F32),
            ],
        ),
        out_shape=[shape((tile_rows, tile_cols), F32), shape((1, tile_rows), F32)],
        compiler_params=pltpu.CompilerParams(vmem_limit_bytes=VMEM),
        name="tile",
    )(
        info, prec_old, feat_r, feat_c, feat_p, got_cols, got_rows, x, mean_p, stats, y, mean_row,
    )
    return updated, mean_next.reshape(tile_rows)


def solution(mesh):
    in_specs = (
        P(("row", "col"), None),
        P(("row", "col")),
        P(("row", "col")),
        P(),
        P(),
        P("row", "col"),
        P("row"),
        P(),
    )
    out_specs = (P("row", "col"), P("row"))
    return jax.shard_map(local, mesh=mesh, in_specs=in_specs, out_specs=out_specs, check_vma=False)
```

```python
import functools

import jax
import jax.numpy as jnp
from jax import lax
from jax.experimental import pallas as pl
from jax.experimental.pallas import tpu as pltpu
from jax.sharding import PartitionSpec as P

PB = 256
RATE = 0.5
EPSILON = 1e-05
SUPER = 64
SUB = 8
WIDE = 16
CHUNK = 512
LANES = 128
VMEM = 62 << 20
F32 = jnp.float32
BF16 = jnp.bfloat16
HIGHEST = lax.Precision.HIGHEST
NN = (((1,), (0,)), ((), ()))
NT = (((1,), (1,)), ((), ()))
TN = (((0,), (0,)), ((), ()))
MESH = pl.DeviceIdType.MESH


def dot(a, b, dims, precision=None):
    return lax.dot_general(a, b, dims, precision=precision, preferred_element_type=F32)


def split_two(x):
    high = x.astype(BF16)
    return high, (x - high.astype(F32)).astype(BF16)


def dot_split(a, b, dims):
    a_high, a_low = a
    b_high, b_low = b
    return dot(a_high, b_high, dims) + (dot(a_high, b_low, dims) + dot(a_low, b_high, dims))


def prep_kernel(
    info, picks_ref, pool_ref, targets_ref, cols_ref, rows_ref, diag_ref, mean_ref, points_ref,
    xs_out, cols_out, rows_out, diag_out, points_out,
):
    in_row = info[2] == 1
    in_col = info[3] == 1
    pool_count = pool_ref.shape[0]
    batch = picks_ref.shape[1]
    ids = lax.broadcasted_iota(jnp.int32, (pool_count, batch), 0)
    chosen_t = jnp.where(ids == picks_ref[...], 1.0, 0.0).astype(BF16)
    eye = jnp.where(
        lax.broadcasted_iota(jnp.int32, (pool_count, pool_count), 0)
        == lax.broadcasted_iota(jnp.int32, (pool_count, pool_count), 1),
        1.0,
        0.0,
    ).astype(BF16)
    chosen = dot(chosen_t, eye, TN)
    values = jnp.sum(chosen * targets_ref[...].astype(F32), axis=1, keepdims=True)
    samples = dot(chosen_t, pool_ref[...], TN)
    width = samples.shape[1]
    xs_out[:, :width] = samples.astype(BF16)
    xs_out[:, width:] = jnp.broadcast_to(values, (batch, LANES)).astype(BF16)
    zero = jnp.float32(0.0)
    cols_out[...] = jnp.where(in_col, cols_ref[...], zero).astype(BF16)
    rows_out[...] = jnp.where(in_row, rows_ref[...], zero).astype(BF16)
    points_out[...] = points_ref[...]
    both = jnp.logical_and(in_row, in_col)
    diag_out[:PB, :] = jnp.where(both, diag_ref[...], zero)
    diag_out[PB:, :] = jnp.where(
        both, jnp.broadcast_to(mean_ref[...], (diag_out.shape[0] - PB, PB)), zero
    )


def feature_block(points, weights, samples_twice, samples_sq):
    scaled = points * weights
    point_sq = jnp.sum(points * scaled, axis=1, keepdims=True)
    high, low = split_two(scaled)
    cross_term = dot(jnp.concatenate([high, low], axis=1), samples_twice, NT)
    return jnp.exp(cross_term - 0.5 * (point_sq + samples_sq))


def eliminate_super(x_ref, base):
    sub_ids = lax.broadcasted_iota(jnp.int32, (SUB, LANES), 0)
    groups = SUPER // SUB
    per = WIDE // SUB
    size = x_ref.shape[0]
    tiles_of = size // LANES
    after = base + SUPER
    for step in range(SUPER // WIDE):
        col0 = base + step * WIDE
        first = step * per
        lane_tiles = [t for t in range(tiles_of) if (t + 1) * LANES > col0]
        lane_tiles += [tiles_of + t for t in range(tiles_of) if t * LANES < col0 + WIDE]
        column = {}
        for g in range(first, groups):
            piece = x_ref[base + g * SUB : base + (g + 1) * SUB, col0 : col0 + WIDE]
            column[g] = [jnp.broadcast_to(piece[:, k : k + 1], (SUB, LANES)) for k in range(WIDE)]
        square = {}
        for k in range(WIDE):
            for m in range(k + 1):
                source = column[first + m // SUB][k]
                square[m, k] = jnp.broadcast_to(
                    source[m % SUB : m % SUB + 1, :], (SUB, LANES)
                )
        scale = []
        below = {}
        for k in range(WIDE):
            scale.append(lax.rsqrt(square[k, k]))
            for j in range(k + 1, WIDE):
                below[j, k] = square[k, j] * scale[k]
            for m in range(k + 1, WIDE):
                for j in range(m, WIDE):
                    square[m, j] = square[m, j] - below[m, k] * below[j, k]
        factor_cols = {}
        for g in range(first, groups):
            for k in range(WIDE):
                if g - first < k // SUB:
                    continue
                value = column[g][k]
                for m in range(k):
                    value = value - factor_cols[g, m] * below[k, m]
                factor_cols[g, k] = value * scale[k]
        for t in lane_tiles:
            lanes = slice(t * LANES, (t + 1) * LANES)
            tiles = {
                g: x_ref[base + g * SUB : base + (g + 1) * SUB, lanes]
                for g in range(first, groups)
            }
            for k in range(WIDE):
                own = first + k // SUB
                at = k % SUB
                pivot_row = jnp.broadcast_to(tiles[own][at : at + 1, :], (SUB, LANES)) * scale[k]
                mine = tiles[own] - jnp.where(sub_ids > at, factor_cols[own, k], 0.0) * pivot_row
                tiles[own] = jnp.where(sub_ids == at, pivot_row, mine)
                for g in range(own + 1, groups):
                    tiles[g] = tiles[g] - factor_cols[g, k] * pivot_row
            for g in tiles:
                x_ref[base + g * SUB : base + (g + 1) * SUB, lanes] = tiles[g]
    if after < size:
        done = x_ref[base:after, after:size]
        for low, high in (
            (after // LANES * LANES, size),
            (size, size + -(-after // LANES) * LANES),
        ):
            x_ref[after:, low:high] = x_ref[after:, low:high] - dot(
                done, x_ref[base:after, low:high], TN, HIGHEST
            )


def move_kernel(
    n_rows, n_cols,
    points_ref, xs_ref, cols_ref, rows_ref, diag_ref, inducing_ref, weights_ref,
    feat_r_out, feat_c_out, feat_p_out, cols_out, rows_out, x_out, mean_out, stats_out, y_out,
    points_c, points_r, feat_r, feat_c, trace_all,
    all_x, diag_got, diag_sum, diag_col, diag_all, cols_got, cols_sum, rows_got, rows_sum, twice,
    send_sem, recv_sem, local_sem,
):
    my_row = lax.axis_index("row")
    my_col = lax.axis_index("col")
    n_of = {"row": n_rows, "col": n_cols}
    me_of = {"row": my_row, "col": my_col}
    slot = [0]

    def peer(axis, distance):
        return lax.rem(me_of[axis] + distance, n_of[axis])

    def peer_id(axis, distance):
        if axis == "row":
            return (peer(axis, distance), my_col)
        return (my_row, peer(axis, distance))

    def send_all(axis, source, target):
        copies = []
        for distance in range(1, n_of[axis]):
            copy = pltpu.make_async_remote_copy(
                src_ref=source(distance),
                dst_ref=target(distance),
                send_sem=send_sem.at[slot[0]],
                recv_sem=recv_sem.at[slot[0]],
                device_id=peer_id(axis, distance),
                device_id_type=MESH,
            )
            slot[0] += 1
            copy.start()
            copies.append(copy)
        return copies

    def arrive(copies):
        for copy in copies:
            copy.wait_recv()

    tile_rows = feat_r.shape[0]
    tile_cols = feat_c.shape[0]
    points_count = inducing_ref.shape[0]
    loads = [
        pltpu.make_async_copy(
            inducing_ref.at[pl.ds(my_col * tile_cols, tile_cols)], points_c, local_sem.at[0]
        ),
        pltpu.make_async_copy(
            inducing_ref.at[pl.ds(my_row * tile_rows, tile_rows)], points_r, local_sem.at[3]
        ),
    ]
    for load in loads:
        load.start()

    barrier = pltpu.get_barrier_semaphore()
    for axis in ("row", "col"):
        for distance in range(1, n_of[axis]):
            pl.semaphore_signal(
                barrier, inc=1, device_id=peer_id(axis, distance), device_id_type=MESH
            )
    pl.semaphore_wait(barrier, n_rows + n_cols - 2)

    batch = xs_ref.shape[0]
    all_x[my_col, my_row] = xs_ref[...]
    xs_first = send_all("row", lambda d: xs_ref, lambda d: all_x.at[my_col, my_row])

    def slices(count, ref, axis):
        return lambda d: ref.at[pl.ds(peer(axis, d) * count, count)]

    def combine(ref, got, axis, count):
        total = ref[pl.ds(me_of[axis] * count, count), :]
        for distance in range(1, n_of[axis]):
            total = total + got[distance - 1]
        return total

    diag_count = diag_sum.shape[0]
    rows_count = rows_sum.shape[0]
    cols_count = cols_sum.shape[0]
    diag_mine = pl.ds(my_row * diag_count, diag_count)
    rows_mine = pl.ds(my_row * rows_count, rows_count)
    cols_mine = pl.ds(my_col * cols_count, cols_count)
    diag_first = send_all(
        "row", slices(diag_count, diag_ref, "row"), lambda d: diag_got.at[d - 1]
    )
    arrive(xs_first)
    xs_second = send_all("col", lambda d: all_x.at[my_col], lambda d: all_x.at[my_col])
    arrive(diag_first)
    diag_sum[...] = combine(diag_ref, diag_got, "row", diag_count)
    diag_second = send_all("col", lambda d: diag_sum, lambda d: diag_col.at[d - 1])
    arrive(xs_second)

    width = inducing_ref.shape[1]
    n_batch = n_rows * n_cols * batch
    gathered = all_x[...].reshape(n_batch, all_x.shape[3])
    samples = gathered[:, :width]
    twice[:, :width] = samples
    twice[:, width:] = samples
    values_t = jnp.transpose(gathered[:, width:].astype(F32))[:SUB, :]
    y_out[...] = values_t.astype(BF16)
    power = jnp.sum(values_t[:1, :] * values_t[:1, :], keepdims=True)
    weights = weights_ref[...]
    samples_f = samples.astype(F32)
    samples_sq = dot(jnp.broadcast_to(weights, (SUB, width)), samples_f * samples_f, NT, HIGHEST)[:1, :]

    def features_of(points):
        return feature_block(points, weights, twice[...], samples_sq)

    step_rows = min(2 * PB, tile_rows, tile_cols)

    def col_step(index, total):
        rows = pl.ds(pl.multiple_of(index * step_rows, step_rows), step_rows)
        exact = features_of(points_c[rows, :])
        feat_c[rows, :] = exact.astype(BF16)
        return total + jnp.sum((exact * exact).reshape(step_rows // SUB, SUB, n_batch), axis=0)

    def row_step(index, carry):
        rows = pl.ds(pl.multiple_of(index * step_rows, step_rows), step_rows)
        feat_r[rows, :] = features_of(points_r[rows, :]).astype(BF16)
        return carry

    loads[0].wait()
    partial = lax.fori_loop(
        0, tile_cols // step_rows, col_step, jnp.zeros((SUB, n_batch), F32)
    )
    trace_all[my_col] = jnp.broadcast_to(jnp.sum(partial, keepdims=True), (SUB, LANES))
    trace_sent = send_all("col", lambda d: trace_all.at[my_col], lambda d: trace_all.at[my_col])
    arrive(diag_second)
    total = diag_sum[...]
    for distance in range(1, n_cols):
        total = total + diag_col[distance - 1]
    diag_all[diag_mine, :] = total
    diag_third = send_all("row", lambda d: diag_all.at[diag_mine], lambda d: diag_all.at[diag_mine])
    cols_first = send_all(
        "col", slices(cols_count, cols_ref, "col"), lambda d: cols_got.at[d - 1]
    )
    rows_first = send_all(
        "row", slices(rows_count, rows_ref, "row"), lambda d: rows_got.at[d - 1]
    )
    loads[1].wait()
    lax.fori_loop(0, tile_rows // step_rows, row_step, 0)
    stores = [
        pltpu.make_async_copy(feat_r, feat_r_out, local_sem.at[1]),
        pltpu.make_async_copy(feat_c, feat_c_out, local_sem.at[2]),
    ]
    for store in stores:
        store.start()
    feat_p = features_of(points_ref[...]).astype(BF16)
    feat_p_out[...] = feat_p
    gram_p = dot(feat_p, feat_p, NT)
    arrive(trace_sent)
    trace_sum = trace_all[0]
    for col in range(1, n_cols):
        trace_sum = trace_sum + trace_all[col]
    trace_scale = trace_sum[:1, :1] / points_count
    gram_scale = RATE / trace_scale
    mean_scale = RATE * lax.rsqrt(trace_scale * (power / n_batch + EPSILON))
    stats_out[0:1, :] = jnp.broadcast_to(gram_scale, (1, LANES))
    stats_out[1:2, :] = jnp.broadcast_to(mean_scale, (1, LANES))
    stats_out[2:, :] = jnp.zeros((SUB - 2, LANES), F32)

    arrive(diag_third)
    mean_out[...] = diag_all[PB : PB + SUB, :]
    x_out[:, :PB] = (1.0 - RATE) * diag_all[:PB, :] + gram_scale * gram_p
    x_out[:, PB:] = jnp.where(
        lax.broadcasted_iota(jnp.int32, (PB, PB), 0) == lax.broadcasted_iota(jnp.int32, (PB, PB), 1),
        1.0,
        0.0,
    )
    for base in range(0, PB, SUPER):
        eliminate_super(x_out, base)
        if base == SUPER:
            arrive(cols_first)
            cols_sum[...] = combine(cols_ref, cols_got, "col", cols_count)
            cols_out[cols_mine, :] = cols_sum[...]
            cols_second = send_all("col", lambda d: cols_sum, lambda d: cols_out.at[cols_mine])
            arrive(rows_first)
            rows_sum[...] = combine(rows_ref, rows_got, "row", rows_count)
            rows_out[rows_mine, :] = rows_sum[...]
            rows_second = send_all("row", lambda d: rows_sum, lambda d: rows_out.at[rows_mine])
    arrive(rows_second)
    arrive(cols_second)
    for copies in (
        xs_first, xs_second, trace_sent, diag_first, diag_second, diag_third,
        rows_first, rows_second, cols_first, cols_second,
    ):
        for copy in copies:
            copy.wait_send()
    for store in stores:
        store.wait()


def tile_kernel(
    info,
    prec_ref, feat_r_ref, feat_c_ref, feat_p_ref, cols_ref, rows_ref, x_ref, mean_p_ref,
    stats_ref, y_ref, mean_ref,
    out_ref, mean_out,
    solved, solved_parts, inverse_high, inverse_low, head,
):
    step = pl.program_id(0)
    in_row = info[2] == 1
    in_col = info[3] == 1
    keep = 1.0 - RATE
    gram_scale = stats_ref[0:1, 0:1]
    mean_scale = stats_ref[1:2, 0:1]

    @pl.when(step == 0)
    def _():
        inverse = x_ref[:, PB:]
        high, low = split_two(inverse)
        inverse_high[...] = high
        inverse_low[...] = low
        joined = keep * rows_ref[...].astype(F32) + gram_scale * dot(feat_p_ref[...], feat_c_ref[...], NT)
        result = dot_split((high, low), split_two(joined), NN)
        solved[...] = result
        result_high, result_low = split_two(result)
        solved_parts[:PB, :] = result_high
        solved_parts[PB : 2 * PB, :] = result_high
        solved_parts[2 * PB :, :] = result_low
        fit = dot(y_ref[...], feat_p_ref[...], NT)
        head[...] = dot(keep * mean_p_ref[...] + mean_scale * fit, inverse, NT, HIGHEST)

    feat_r = feat_r_ref[...]
    piece = keep * cols_ref[...].astype(F32) + gram_scale * dot(feat_r, feat_p_ref[...], NT)
    wide = dot_split(split_two(piece), (inverse_high[...], inverse_low[...]), NT)
    wide_high, wide_low = split_two(wide)
    wide_parts = jnp.concatenate([wide_high, wide_low, wide_high], axis=1)
    for low in range(0, prec_ref.shape[1], CHUNK):
        lanes = slice(low, low + CHUNK)
        gram = dot(feat_r, feat_c_ref[lanes, :], NT)
        out_ref[:, lanes] = (keep * prec_ref[:, lanes] + gram_scale * gram) - dot(
            wide_parts, solved_parts[:, lanes], NN
        )
    fit = dot(y_ref[...], feat_r, NT)
    mean_next = (
        keep * mean_ref[...] + mean_scale * fit[:1, :] - dot_split(split_two(head[...]), (wide_high, wide_low), NT)[:1, :]
    )
    mean_out[...] = mean_next
    col0 = pl.multiple_of(info[1] * PB, PB)

    @pl.when(in_col)
    def _():
        out_ref[:, pl.ds(col0, PB)] = wide

    here = jnp.logical_and(in_row, step == info[0])

    @pl.when(here)
    def _():
        out_ref[...] = solved[...]
        mean_out[...] = head[:1, :]

    @pl.when(jnp.logical_and(here, in_col))
    def _():
        factor = jnp.transpose(x_ref[:, :PB])
        lower = lax.broadcasted_iota(jnp.int32, (PB, PB), 0) >= lax.broadcasted_iota(
            jnp.int32, (PB, PB), 1
        )
        out_ref[:, pl.ds(col0, PB)] = jnp.where(lower, factor, 0.0)


def whole(memory=pltpu.VMEM):
    return pl.BlockSpec(memory_space=memory)


def local(pool, targets, picks, inducing, inv_sq_lengths, prec_old, mean_old, panel):
    n_rows = lax.axis_size("row")
    n_cols = lax.axis_size("col")
    my_row = lax.axis_index("row")
    my_col = lax.axis_index("col")
    tile_rows, tile_cols = prec_old.shape
    batch = picks.shape[0]
    n_batch = batch * n_rows * n_cols
    width = pool.shape[1]
    row_blocks = tile_rows // PB
    col_blocks = tile_cols // PB
    index = panel[0]
    info = jnp.stack(
        [
            lax.rem(index, row_blocks),
            lax.rem(index, col_blocks),
            (index // row_blocks == my_row).astype(jnp.int32),
            (index // col_blocks == my_col).astype(jnp.int32),
            index,
        ]
    )
    mean_row = mean_old.reshape(1, tile_rows)
    shape = jax.ShapeDtypeStruct
    diag_count = -(-(PB + SUB) // (n_rows * SUB)) * SUB
    diag_rows = diag_count * n_rows
    full = lambda *dims: pl.BlockSpec(dims, lambda i, info: (0,) * len(dims))
    xs, cols, rows, diag, points = pl.pallas_call(
        prep_kernel,
        grid_spec=pltpu.PrefetchScalarGridSpec(
            num_scalar_prefetch=1,
            grid=(1,),
            in_specs=[
                full(1, batch),
                full(*pool.shape),
                full(1, pool.shape[0]),
                pl.BlockSpec((tile_rows, PB), lambda i, info: (0, info[1])),
                pl.BlockSpec((PB, tile_cols), lambda i, info: (info[0], 0)),
                pl.BlockSpec((PB, PB), lambda i, info: (info[0], info[1])),
                pl.BlockSpec((1, PB), lambda i, info: (0, info[0])),
                pl.BlockSpec((PB, width), lambda i, info: (info[4], 0)),
            ],
            out_specs=[
                full(batch, width + LANES),
                full(tile_rows, PB),
                full(PB, tile_cols),
                full(diag_rows, PB),
                full(PB, width),
            ],
        ),
        out_shape=[
            shape((batch, width + LANES), BF16),
            shape((tile_rows, PB), BF16),
            shape((PB, tile_cols), BF16),
            shape((diag_rows, PB), F32),
            shape((PB, width), F32),
        ],
        compiler_params=pltpu.CompilerParams(vmem_limit_bytes=VMEM),
        name="prep",
    )(
        info, picks.reshape(1, batch), pool, targets.reshape(1, -1),
        prec_old, prec_old, prec_old, mean_row, inducing,
    )
    sems = 5 * (n_rows - 1) + 5 * (n_cols - 1)
    cols_count = tile_rows // n_cols
    rows_count = PB // n_rows
    moved = pl.pallas_call(
        functools.partial(move_kernel, n_rows, n_cols),
        in_specs=[whole()] * 5 + [whole(pl.ANY), whole()],
        out_specs=[whole(pl.ANY)] * 2 + [whole()] * 7,
        out_shape=[
            shape((tile_rows, n_batch), BF16),
            shape((tile_cols, n_batch), BF16),
            shape((PB, n_batch), BF16),
            shape((tile_rows, PB), BF16),
            shape((PB, tile_cols), BF16),
            shape((PB, 2 * PB), F32),
            shape((SUB, PB), F32),
            shape((SUB, LANES), F32),
            shape((SUB, n_batch), BF16),
        ],
        scratch_shapes=[
            pltpu.VMEM((tile_cols, width), F32),
            pltpu.VMEM((tile_rows, width), F32),
            pltpu.VMEM((tile_rows, n_batch), BF16),
            pltpu.VMEM((tile_cols, n_batch), BF16),
            pltpu.VMEM((n_cols, SUB, LANES), F32),
            pltpu.VMEM((n_cols, n_rows, batch, width + LANES), BF16),
            pltpu.VMEM((n_rows - 1, diag_count, PB), F32),
            pltpu.VMEM((diag_count, PB), F32),
            pltpu.VMEM((n_cols - 1, diag_count, PB), F32),
            pltpu.VMEM((diag_rows, PB), F32),
            pltpu.VMEM((n_cols - 1, cols_count, PB), BF16),
            pltpu.VMEM((cols_count, PB), BF16),
            pltpu.VMEM((n_rows - 1, rows_count, tile_cols), BF16),
            pltpu.VMEM((rows_count, tile_cols), BF16),
            pltpu.VMEM((n_batch, 2 * width), BF16),
            pltpu.SemaphoreType.DMA((sems,)),
            pltpu.SemaphoreType.DMA((sems,)),
            pltpu.SemaphoreType.DMA((4,)),
        ],
        compiler_params=pltpu.CompilerParams(
            collective_id=0, has_side_effects=True, vmem_limit_bytes=VMEM
        ),
        name="move",
    )(points, xs, cols, rows, diag, inducing, inv_sq_lengths.reshape(1, width))
    feat_r, feat_c, feat_p, got_cols, got_rows, x, mean_p, stats, y = moved
    step_rows = PB
    updated, mean_next = pl.pallas_call(
        tile_kernel,
        grid_spec=pltpu.PrefetchScalarGridSpec(
            num_scalar_prefetch=1,
            grid=(tile_rows // step_rows,),
            in_specs=[
                pl.BlockSpec((step_rows, tile_cols), lambda i, info: (i, 0)),
                pl.BlockSpec((step_rows, n_batch), lambda i, info: (i, 0)),
                full(tile_cols, n_batch),
                full(PB, n_batch),
                pl.BlockSpec((step_rows, PB), lambda i, info: (i, 0)),
                full(PB, tile_cols),
                full(PB, 2 * PB),
                full(SUB, PB),
                full(SUB, LANES),
                full(SUB, n_batch),
                pl.BlockSpec((1, step_rows), lambda i, info: (0, i)),
            ],
            out_specs=[
                pl.BlockSpec((step_rows, tile_cols), lambda i, info: (i, 0)),
                pl.BlockSpec((1, step_rows), lambda i, info: (0, i)),
            ],
            scratch_shapes=[
                pltpu.VMEM((PB, tile_cols), F32),
                pltpu.VMEM((3 * PB, tile_cols), BF16),
                pltpu.VMEM((PB, PB), BF16),
                pltpu.VMEM((PB, PB), BF16),
                pltpu.VMEM((SUB, PB), F32),
            ],
        ),
        out_shape=[shape((tile_rows, tile_cols), F32), shape((1, tile_rows), F32)],
        compiler_params=pltpu.CompilerParams(vmem_limit_bytes=VMEM),
        name="tile",
    )(
        info, prec_old, feat_r, feat_c, feat_p, got_cols, got_rows, x, mean_p, stats, y, mean_row,
    )
    return updated, mean_next.reshape(tile_rows)


def solution(mesh):
    in_specs = (
        P(("row", "col"), None),
        P(("row", "col")),
        P(("row", "col")),
        P(),
        P(),
        P("row", "col"),
        P("row"),
        P(),
    )
    out_specs = (P("row", "col"), P("row"))
    return jax.shard_map(local, mesh=mesh, in_specs=in_specs, out_specs=out_specs, check_vma=False)
```

```python
import functools

import jax
import jax.numpy as jnp
from jax import lax
from jax.experimental import pallas as pl
from jax.experimental.pallas import tpu as pltpu
from jax.sharding import PartitionSpec as P

PB = 256
RATE = 0.5
EPSILON = 1e-05
SUPER = 64
SUB = 8
WIDE = 8
CHUNK = 512
PREP = 4
LANES = 128
VMEM = 62 << 20
F32 = jnp.float32
BF16 = jnp.bfloat16
HIGHEST = lax.Precision.HIGHEST
NN = (((1,), (0,)), ((), ()))
NT = (((1,), (1,)), ((), ()))
TN = (((0,), (0,)), ((), ()))
MESH = pl.DeviceIdType.MESH


def dot(a, b, dims, precision=None):
    return lax.dot_general(a, b, dims, precision=precision, preferred_element_type=F32)


def split_two(x):
    high = x.astype(BF16)
    return high, (x - high.astype(F32)).astype(BF16)


def dot_split(a, b, dims):
    a_high, a_low = a
    b_high, b_low = b
    return dot(a_high, b_high, dims) + (dot(a_high, b_low, dims) + dot(a_low, b_high, dims))


def prep_kernel(
    info, picks_ref, pool_ref, targets_ref, cols_ref, rows_ref, diag_ref, mean_ref, points_ref,
    xs_out, cols_out, rows_out, diag_out, points_out,
):
    in_row = info[2] == 1
    in_col = info[3] == 1
    zero = jnp.float32(0.0)
    cols_out[...] = jnp.where(in_col, cols_ref[...], zero).astype(BF16)
    rows_out[...] = jnp.where(in_row, rows_ref[...], zero).astype(BF16)
    first = pl.program_id(0) == 0

    @pl.when(first)
    def _():
        prep_small(
            in_row, in_col, picks_ref, pool_ref, targets_ref, diag_ref, mean_ref, points_ref,
            xs_out, diag_out, points_out,
        )


def prep_small(
    in_row, in_col, picks_ref, pool_ref, targets_ref, diag_ref, mean_ref, points_ref,
    xs_out, diag_out, points_out,
):
    pool_count = pool_ref.shape[0]
    batch = picks_ref.shape[1]
    ids = lax.broadcasted_iota(jnp.int32, (pool_count, batch), 0)
    chosen_t = jnp.where(ids == picks_ref[...], 1.0, 0.0).astype(BF16)
    eye = jnp.where(
        lax.broadcasted_iota(jnp.int32, (pool_count, pool_count), 0)
        == lax.broadcasted_iota(jnp.int32, (pool_count, pool_count), 1),
        1.0,
        0.0,
    ).astype(BF16)
    chosen = dot(chosen_t, eye, TN)
    values = jnp.sum(chosen * targets_ref[...].astype(F32), axis=1, keepdims=True)
    samples = dot(chosen_t, pool_ref[...], TN)
    width = samples.shape[1]
    xs_out[:, :width] = samples.astype(BF16)
    xs_out[:, width:] = jnp.broadcast_to(values, (batch, LANES)).astype(BF16)
    zero = jnp.float32(0.0)
    points_out[...] = points_ref[...]
    both = jnp.logical_and(in_row, in_col)
    diag_out[:PB, :] = jnp.where(both, diag_ref[...], zero)
    diag_out[PB:, :] = jnp.where(
        both, jnp.broadcast_to(mean_ref[...], (diag_out.shape[0] - PB, PB)), zero
    )


def feature_block(points, weights, samples_twice, samples_sq):
    scaled = points * weights
    point_sq = jnp.sum(points * scaled, axis=1, keepdims=True)
    high, low = split_two(scaled)
    cross_term = dot(jnp.concatenate([high, low], axis=1), samples_twice, NT)
    return jnp.exp(cross_term - 0.5 * (point_sq + samples_sq))


def eliminate_super(x_ref, base):
    sub_ids = lax.broadcasted_iota(jnp.int32, (SUB, LANES), 0)
    groups = SUPER // SUB
    per = WIDE // SUB
    size = x_ref.shape[0]
    tiles_of = size // LANES
    after = base + SUPER
    for step in range(SUPER // WIDE):
        col0 = base + step * WIDE
        first = step * per
        lane_tiles = [t for t in range(tiles_of) if (t + 1) * LANES > col0]
        lane_tiles += [tiles_of + t for t in range(tiles_of) if t * LANES < col0 + WIDE]
        column = {}
        for g in range(first, groups):
            piece = x_ref[base + g * SUB : base + (g + 1) * SUB, col0 : col0 + WIDE]
            column[g] = [jnp.broadcast_to(piece[:, k : k + 1], (SUB, LANES)) for k in range(WIDE)]
        square = {}
        for k in range(WIDE):
            for m in range(k + 1):
                source = column[first + m // SUB][k]
                square[m, k] = jnp.broadcast_to(
                    source[m % SUB : m % SUB + 1, :], (SUB, LANES)
                )
        scale = []
        below = {}
        for k in range(WIDE):
            scale.append(lax.rsqrt(square[k, k]))
            for j in range(k + 1, WIDE):
                below[j, k] = square[k, j] * scale[k]
            for m in range(k + 1, WIDE):
                for j in range(m, WIDE):
                    square[m, j] = square[m, j] - below[m, k] * below[j, k]
        factor_cols = {}
        for g in range(first, groups):
            for k in range(WIDE):
                if g - first < k // SUB:
                    continue
                value = column[g][k]
                for m in range(k):
                    value = value - factor_cols[g, m] * below[k, m]
                factor_cols[g, k] = value * scale[k]
        for t in lane_tiles:
            lanes = slice(t * LANES, (t + 1) * LANES)
            tiles = {
                g: x_ref[base + g * SUB : base + (g + 1) * SUB, lanes]
                for g in range(first, groups)
            }
            for k in range(WIDE):
                own = first + k // SUB
                at = k % SUB
                pivot_row = jnp.broadcast_to(tiles[own][at : at + 1, :], (SUB, LANES)) * scale[k]
                mine = tiles[own] - jnp.where(sub_ids > at, factor_cols[own, k], 0.0) * pivot_row
                tiles[own] = jnp.where(sub_ids == at, pivot_row, mine)
                for g in range(own + 1, groups):
                    tiles[g] = tiles[g] - factor_cols[g, k] * pivot_row
            for g in tiles:
                x_ref[base + g * SUB : base + (g + 1) * SUB, lanes] = tiles[g]
    if after < size:
        done = x_ref[base:after, after:size]
        for low, high in (
            (after // LANES * LANES, size),
            (size, size + -(-after // LANES) * LANES),
        ):
            x_ref[after:, low:high] = x_ref[after:, low:high] - dot(
                done, x_ref[base:after, low:high], TN, HIGHEST
            )


def move_kernel(
    n_rows, n_cols,
    points_ref, xs_ref, cols_ref, rows_ref, diag_ref, inducing_ref, weights_ref,
    feat_r_out, feat_c_out, feat_p_out, cols_out, rows_out, x_out, mean_out, stats_out, y_out,
    points_c, points_r, feat_r, feat_c, trace_all,
    all_x, diag_got, diag_sum, diag_col, diag_all, cols_got, cols_sum, rows_got, rows_sum, twice,
    send_sem, recv_sem, local_sem,
):
    my_row = lax.axis_index("row")
    my_col = lax.axis_index("col")
    n_of = {"row": n_rows, "col": n_cols}
    me_of = {"row": my_row, "col": my_col}
    slot = [0]

    def peer(axis, distance):
        return lax.rem(me_of[axis] + distance, n_of[axis])

    def peer_id(axis, distance):
        if axis == "row":
            return (peer(axis, distance), my_col)
        return (my_row, peer(axis, distance))

    def send_all(axis, source, target):
        copies = []
        for distance in range(1, n_of[axis]):
            copy = pltpu.make_async_remote_copy(
                src_ref=source(distance),
                dst_ref=target(distance),
                send_sem=send_sem.at[slot[0]],
                recv_sem=recv_sem.at[slot[0]],
                device_id=peer_id(axis, distance),
                device_id_type=MESH,
            )
            slot[0] += 1
            copy.start()
            copies.append(copy)
        return copies

    def arrive(copies):
        for copy in copies:
            copy.wait_recv()

    tile_rows = feat_r.shape[0]
    tile_cols = feat_c.shape[0]
    points_count = inducing_ref.shape[0]
    loads = [
        pltpu.make_async_copy(
            inducing_ref.at[pl.ds(my_col * tile_cols, tile_cols)], points_c, local_sem.at[0]
        ),
        pltpu.make_async_copy(
            inducing_ref.at[pl.ds(my_row * tile_rows, tile_rows)], points_r, local_sem.at[3]
        ),
    ]
    for load in loads:
        load.start()

    barrier = pltpu.get_barrier_semaphore()
    for axis in ("row", "col"):
        for distance in range(1, n_of[axis]):
            pl.semaphore_signal(
                barrier, inc=1, device_id=peer_id(axis, distance), device_id_type=MESH
            )
    pl.semaphore_wait(barrier, n_rows + n_cols - 2)

    batch = xs_ref.shape[0]
    all_x[my_col, my_row] = xs_ref[...]
    xs_first = send_all("row", lambda d: xs_ref, lambda d: all_x.at[my_col, my_row])

    def slices(count, ref, axis):
        return lambda d: ref.at[pl.ds(peer(axis, d) * count, count)]

    def combine(ref, got, axis, count):
        total = ref[pl.ds(me_of[axis] * count, count), :]
        for distance in range(1, n_of[axis]):
            total = total + got[distance - 1]
        return total

    diag_count = diag_sum.shape[0]
    rows_count = rows_sum.shape[0]
    cols_count = cols_sum.shape[0]
    diag_mine = pl.ds(my_row * diag_count, diag_count)
    rows_mine = pl.ds(my_row * rows_count, rows_count)
    cols_mine = pl.ds(my_col * cols_count, cols_count)
    diag_first = send_all(
        "row", slices(diag_count, diag_ref, "row"), lambda d: diag_got.at[d - 1]
    )
    arrive(xs_first)
    xs_second = send_all("col", lambda d: all_x.at[my_col], lambda d: all_x.at[my_col])
    cols_first = send_all(
        "col", slices(cols_count, cols_ref, "col"), lambda d: cols_got.at[d - 1]
    )
    arrive(diag_first)
    diag_sum[...] = combine(diag_ref, diag_got, "row", diag_count)
    diag_second = send_all("col", lambda d: diag_sum, lambda d: diag_col.at[d - 1])
    rows_first = send_all(
        "row", slices(rows_count, rows_ref, "row"), lambda d: rows_got.at[d - 1]
    )
    arrive(xs_second)

    width = inducing_ref.shape[1]
    n_batch = n_rows * n_cols * batch
    gathered = all_x[...].reshape(n_batch, all_x.shape[3])
    samples = gathered[:, :width]
    twice[:, :width] = samples
    twice[:, width:] = samples
    values_t = jnp.transpose(gathered[:, width:].astype(F32))[:SUB, :]
    y_out[...] = values_t.astype(BF16)
    power = jnp.sum(values_t[:1, :] * values_t[:1, :], keepdims=True)
    weights = weights_ref[...]
    samples_f = samples.astype(F32)
    samples_sq = dot(jnp.broadcast_to(weights, (SUB, width)), samples_f * samples_f, NT, HIGHEST)[:1, :]

    def features_of(points):
        return feature_block(points, weights, twice[...], samples_sq)

    step_rows = min(2 * PB, tile_rows, tile_cols)

    def col_step(index, total):
        rows = pl.ds(pl.multiple_of(index * step_rows, step_rows), step_rows)
        exact = features_of(points_c[rows, :])
        feat_c[rows, :] = exact.astype(BF16)
        return total + jnp.sum((exact * exact).reshape(step_rows // SUB, SUB, n_batch), axis=0)

    def row_step(index, carry):
        rows = pl.ds(pl.multiple_of(index * step_rows, step_rows), step_rows)
        feat_r[rows, :] = features_of(points_r[rows, :]).astype(BF16)
        return carry

    loads[0].wait()
    partial = lax.fori_loop(
        0, tile_cols // step_rows, col_step, jnp.zeros((SUB, n_batch), F32)
    )
    trace_all[my_col] = jnp.broadcast_to(jnp.sum(partial, keepdims=True), (SUB, LANES))
    trace_sent = send_all("col", lambda d: trace_all.at[my_col], lambda d: trace_all.at[my_col])
    arrive(diag_second)
    total = diag_sum[...]
    for distance in range(1, n_cols):
        total = total + diag_col[distance - 1]
    diag_all[diag_mine, :] = total
    diag_third = send_all("row", lambda d: diag_all.at[diag_mine], lambda d: diag_all.at[diag_mine])
    loads[1].wait()
    lax.fori_loop(0, tile_rows // step_rows, row_step, 0)
    stores = [
        pltpu.make_async_copy(feat_r, feat_r_out, local_sem.at[1]),
        pltpu.make_async_copy(feat_c, feat_c_out, local_sem.at[2]),
    ]
    for store in stores:
        store.start()
    feat_p = features_of(points_ref[...]).astype(BF16)
    feat_p_out[...] = feat_p
    gram_p = dot(feat_p, feat_p, NT)
    arrive(trace_sent)
    trace_sum = trace_all[0]
    for col in range(1, n_cols):
        trace_sum = trace_sum + trace_all[col]
    trace_scale = trace_sum[:1, :1] / points_count
    gram_scale = RATE / trace_scale
    mean_scale = RATE * lax.rsqrt(trace_scale * (power / n_batch + EPSILON))
    stats_out[0:1, :] = jnp.broadcast_to(gram_scale, (1, LANES))
    stats_out[1:2, :] = jnp.broadcast_to(mean_scale, (1, LANES))
    stats_out[2:, :] = jnp.zeros((SUB - 2, LANES), F32)

    arrive(diag_third)
    mean_out[...] = diag_all[PB : PB + SUB, :]
    x_out[:, :PB] = (1.0 - RATE) * diag_all[:PB, :] + gram_scale * gram_p
    x_out[:, PB:] = jnp.where(
        lax.broadcasted_iota(jnp.int32, (PB, PB), 0) == lax.broadcasted_iota(jnp.int32, (PB, PB), 1),
        1.0,
        0.0,
    )
    for base in range(0, PB, SUPER):
        eliminate_super(x_out, base)
        if base == 0:
            arrive(cols_first)
            cols_sum[...] = combine(cols_ref, cols_got, "col", cols_count)
            cols_out[cols_mine, :] = cols_sum[...]
            cols_second = send_all("col", lambda d: cols_sum, lambda d: cols_out.at[cols_mine])
            arrive(rows_first)
            rows_sum[...] = combine(rows_ref, rows_got, "row", rows_count)
            rows_out[rows_mine, :] = rows_sum[...]
            rows_second = send_all("row", lambda d: rows_sum, lambda d: rows_out.at[rows_mine])
    arrive(rows_second)
    arrive(cols_second)
    for copies in (
        xs_first, xs_second, trace_sent, diag_first, diag_second, diag_third,
        rows_first, rows_second, cols_first, cols_second,
    ):
        for copy in copies:
            copy.wait_send()
    for store in stores:
        store.wait()


def tile_kernel(
    info,
    prec_ref, feat_r_ref, feat_c_ref, feat_p_ref, cols_ref, rows_ref, x_ref, mean_p_ref,
    stats_ref, y_ref, mean_ref,
    out_ref, mean_out,
    solved, solved_parts, inverse_high, inverse_low, head,
):
    step = pl.program_id(0)
    in_row = info[2] == 1
    in_col = info[3] == 1
    keep = 1.0 - RATE
    gram_scale = stats_ref[0:1, 0:1]
    mean_scale = stats_ref[1:2, 0:1]

    @pl.when(step == 0)
    def _():
        inverse = x_ref[:, PB:]
        high, low = split_two(inverse)
        inverse_high[...] = high
        inverse_low[...] = low
        joined = keep * rows_ref[...].astype(F32) + gram_scale * dot(feat_p_ref[...], feat_c_ref[...], NT)
        result = dot_split((high, low), split_two(joined), NN)
        solved[...] = result
        result_high, result_low = split_two(result)
        solved_parts[:PB, :] = result_high
        solved_parts[PB : 2 * PB, :] = result_high
        solved_parts[2 * PB :, :] = result_low
        fit = dot(y_ref[...], feat_p_ref[...], NT)
        head[...] = dot(keep * mean_p_ref[...] + mean_scale * fit, inverse, NT, HIGHEST)

    feat_r = feat_r_ref[...]
    piece = keep * cols_ref[...].astype(F32) + gram_scale * dot(feat_r, feat_p_ref[...], NT)
    wide = dot_split(split_two(piece), (inverse_high[...], inverse_low[...]), NT)
    wide_high, wide_low = split_two(wide)
    wide_parts = jnp.concatenate([wide_high, wide_low, wide_high], axis=1)
    for low in range(0, prec_ref.shape[1], CHUNK):
        lanes = slice(low, low + CHUNK)
        gram = dot(feat_r, feat_c_ref[lanes, :], NT)
        out_ref[:, lanes] = (keep * prec_ref[:, lanes] + gram_scale * gram) - dot(
            wide_parts, solved_parts[:, lanes], NN
        )
    fit = dot(y_ref[...], feat_r, NT)
    mean_next = (
        keep * mean_ref[...] + mean_scale * fit[:1, :] - dot_split(split_two(head[...]), (wide_high, wide_low), NT)[:1, :]
    )
    mean_out[...] = mean_next
    col0 = pl.multiple_of(info[1] * PB, PB)

    @pl.when(in_col)
    def _():
        out_ref[:, pl.ds(col0, PB)] = wide

    here = jnp.logical_and(in_row, step == info[0])

    @pl.when(here)
    def _():
        out_ref[...] = solved[...]
        mean_out[...] = head[:1, :]

    @pl.when(jnp.logical_and(here, in_col))
    def _():
        factor = jnp.transpose(x_ref[:, :PB])
        lower = lax.broadcasted_iota(jnp.int32, (PB, PB), 0) >= lax.broadcasted_iota(
            jnp.int32, (PB, PB), 1
        )
        out_ref[:, pl.ds(col0, PB)] = jnp.where(lower, factor, 0.0)


def whole(memory=pltpu.VMEM):
    return pl.BlockSpec(memory_space=memory)


def local(pool, targets, picks, inducing, inv_sq_lengths, prec_old, mean_old, panel):
    n_rows = lax.axis_size("row")
    n_cols = lax.axis_size("col")
    my_row = lax.axis_index("row")
    my_col = lax.axis_index("col")
    tile_rows, tile_cols = prec_old.shape
    batch = picks.shape[0]
    n_batch = batch * n_rows * n_cols
    width = pool.shape[1]
    row_blocks = tile_rows // PB
    col_blocks = tile_cols // PB
    index = panel[0]
    info = jnp.stack(
        [
            lax.rem(index, row_blocks),
            lax.rem(index, col_blocks),
            (index // row_blocks == my_row).astype(jnp.int32),
            (index // col_blocks == my_col).astype(jnp.int32),
            index,
        ]
    )
    mean_row = mean_old.reshape(1, tile_rows)
    shape = jax.ShapeDtypeStruct
    diag_count = -(-(PB + SUB) // (n_rows * SUB)) * SUB
    diag_rows = diag_count * n_rows
    full = lambda *dims: pl.BlockSpec(dims, lambda i, info: (0,) * len(dims))
    xs, cols, rows, diag, points = pl.pallas_call(
        prep_kernel,
        grid_spec=pltpu.PrefetchScalarGridSpec(
            num_scalar_prefetch=1,
            grid=(PREP,),
            in_specs=[
                full(1, batch),
                full(*pool.shape),
                full(1, pool.shape[0]),
                pl.BlockSpec((tile_rows // PREP, PB), lambda i, info: (i, info[1])),
                pl.BlockSpec((PB, tile_cols // PREP), lambda i, info: (info[0], i)),
                pl.BlockSpec((PB, PB), lambda i, info: (info[0], info[1])),
                pl.BlockSpec((1, PB), lambda i, info: (0, info[0])),
                pl.BlockSpec((PB, width), lambda i, info: (info[4], 0)),
            ],
            out_specs=[
                full(batch, width + LANES),
                pl.BlockSpec((tile_rows // PREP, PB), lambda i, info: (i, 0)),
                pl.BlockSpec((PB, tile_cols // PREP), lambda i, info: (0, i)),
                full(diag_rows, PB),
                full(PB, width),
            ],
        ),
        out_shape=[
            shape((batch, width + LANES), BF16),
            shape((tile_rows, PB), BF16),
            shape((PB, tile_cols), BF16),
            shape((diag_rows, PB), F32),
            shape((PB, width), F32),
        ],
        compiler_params=pltpu.CompilerParams(vmem_limit_bytes=VMEM),
        name="prep",
    )(
        info, picks.reshape(1, batch), pool, targets.reshape(1, -1),
        prec_old, prec_old, prec_old, mean_row, inducing,
    )
    sems = 5 * (n_rows - 1) + 5 * (n_cols - 1)
    cols_count = tile_rows // n_cols
    rows_count = PB // n_rows
    moved = pl.pallas_call(
        functools.partial(move_kernel, n_rows, n_cols),
        in_specs=[whole()] * 5 + [whole(pl.ANY), whole()],
        out_specs=[whole(pl.ANY)] * 2 + [whole()] * 7,
        out_shape=[
            shape((tile_rows, n_batch), BF16),
            shape((tile_cols, n_batch), BF16),
            shape((PB, n_batch), BF16),
            shape((tile_rows, PB), BF16),
            shape((PB, tile_cols), BF16),
            shape((PB, 2 * PB), F32),
            shape((SUB, PB), F32),
            shape((SUB, LANES), F32),
            shape((SUB, n_batch), BF16),
        ],
        scratch_shapes=[
            pltpu.VMEM((tile_cols, width), F32),
            pltpu.VMEM((tile_rows, width), F32),
            pltpu.VMEM((tile_rows, n_batch), BF16),
            pltpu.VMEM((tile_cols, n_batch), BF16),
            pltpu.VMEM((n_cols, SUB, LANES), F32),
            pltpu.VMEM((n_cols, n_rows, batch, width + LANES), BF16),
            pltpu.VMEM((n_rows - 1, diag_count, PB), F32),
            pltpu.VMEM((diag_count, PB), F32),
            pltpu.VMEM((n_cols - 1, diag_count, PB), F32),
            pltpu.VMEM((diag_rows, PB), F32),
            pltpu.VMEM((n_cols - 1, cols_count, PB), BF16),
            pltpu.VMEM((cols_count, PB), BF16),
            pltpu.VMEM((n_rows - 1, rows_count, tile_cols), BF16),
            pltpu.VMEM((rows_count, tile_cols), BF16),
            pltpu.VMEM((n_batch, 2 * width), BF16),
            pltpu.SemaphoreType.DMA((sems,)),
            pltpu.SemaphoreType.DMA((sems,)),
            pltpu.SemaphoreType.DMA((4,)),
        ],
        compiler_params=pltpu.CompilerParams(
            collective_id=0, has_side_effects=True, vmem_limit_bytes=VMEM
        ),
        name="move",
    )(points, xs, cols, rows, diag, inducing, inv_sq_lengths.reshape(1, width))
    feat_r, feat_c, feat_p, got_cols, got_rows, x, mean_p, stats, y = moved
    step_rows = PB
    updated, mean_next = pl.pallas_call(
        tile_kernel,
        grid_spec=pltpu.PrefetchScalarGridSpec(
            num_scalar_prefetch=1,
            grid=(tile_rows // step_rows,),
            in_specs=[
                pl.BlockSpec((step_rows, tile_cols), lambda i, info: (i, 0)),
                pl.BlockSpec((step_rows, n_batch), lambda i, info: (i, 0)),
                full(tile_cols, n_batch),
                full(PB, n_batch),
                pl.BlockSpec((step_rows, PB), lambda i, info: (i, 0)),
                full(PB, tile_cols),
                full(PB, 2 * PB),
                full(SUB, PB),
                full(SUB, LANES),
                full(SUB, n_batch),
                pl.BlockSpec((1, step_rows), lambda i, info: (0, i)),
            ],
            out_specs=[
                pl.BlockSpec((step_rows, tile_cols), lambda i, info: (i, 0)),
                pl.BlockSpec((1, step_rows), lambda i, info: (0, i)),
            ],
            scratch_shapes=[
                pltpu.VMEM((PB, tile_cols), F32),
                pltpu.VMEM((3 * PB, tile_cols), BF16),
                pltpu.VMEM((PB, PB), BF16),
                pltpu.VMEM((PB, PB), BF16),
                pltpu.VMEM((SUB, PB), F32),
            ],
        ),
        out_shape=[shape((tile_rows, tile_cols), F32), shape((1, tile_rows), F32)],
        compiler_params=pltpu.CompilerParams(vmem_limit_bytes=VMEM),
        name="tile",
    )(
        info, prec_old, feat_r, feat_c, feat_p, got_cols, got_rows, x, mean_p, stats, y, mean_row,
    )
    return updated, mean_next.reshape(tile_rows)


def solution(mesh):
    in_specs = (
        P(("row", "col"), None),
        P(("row", "col")),
        P(("row", "col")),
        P(),
        P(),
        P("row", "col"),
        P("row"),
        P(),
    )
    out_specs = (P("row", "col"), P("row"))
    return jax.shard_map(local, mesh=mesh, in_specs=in_specs, out_specs=out_specs, check_vma=False)
```

```python
import functools

import jax
import jax.numpy as jnp
from jax import lax
from jax.experimental import pallas as pl
from jax.experimental.pallas import tpu as pltpu
from jax.sharding import PartitionSpec as P

PB = 256
RATE = 0.5
EPSILON = 1e-05
SUPER = 64
SUB = 8
WIDE = 8
CHUNK = 512
LANES = 128
VMEM = 62 << 20
F32 = jnp.float32
BF16 = jnp.bfloat16
HIGHEST = lax.Precision.HIGHEST
NN = (((1,), (0,)), ((), ()))
NT = (((1,), (1,)), ((), ()))
TN = (((0,), (0,)), ((), ()))
MESH = pl.DeviceIdType.MESH


def dot(a, b, dims, precision=None):
    return lax.dot_general(a, b, dims, precision=precision, preferred_element_type=F32)


def split_two(x):
    high = x.astype(BF16)
    return high, (x - high.astype(F32)).astype(BF16)


def dot_split(a, b, dims):
    a_high, a_low = a
    b_high, b_low = b
    return dot(a_high, b_high, dims) + (dot(a_high, b_low, dims) + dot(a_low, b_high, dims))


def prep_kernel(
    info, picks_ref, pool_ref, targets_ref, cols_ref, rows_ref, diag_ref, mean_ref, points_ref,
    xs_out, cols_out, rows_out, diag_out, points_out,
):
    in_row = info[2] == 1
    in_col = info[3] == 1
    pool_count = pool_ref.shape[0]
    batch = picks_ref.shape[1]
    ids = lax.broadcasted_iota(jnp.int32, (pool_count, batch), 0)
    chosen_t = jnp.where(ids == picks_ref[...], 1.0, 0.0).astype(BF16)
    eye = jnp.where(
        lax.broadcasted_iota(jnp.int32, (pool_count, pool_count), 0)
        == lax.broadcasted_iota(jnp.int32, (pool_count, pool_count), 1),
        1.0,
        0.0,
    ).astype(BF16)
    chosen = dot(chosen_t, eye, TN)
    values = jnp.sum(chosen * targets_ref[...].astype(F32), axis=1, keepdims=True)
    samples = dot(chosen_t, pool_ref[...], TN)
    width = samples.shape[1]
    xs_out[:, :width] = samples.astype(BF16)
    xs_out[:, width:] = jnp.broadcast_to(values, (batch, LANES)).astype(BF16)
    zero = jnp.float32(0.0)
    cols_out[...] = jnp.where(in_col, cols_ref[...], zero).astype(BF16)
    rows_out[...] = jnp.where(in_row, rows_ref[...], zero).astype(BF16)
    points_out[...] = points_ref[...]
    both = jnp.logical_and(in_row, in_col)
    diag_out[:PB, :] = jnp.where(both, diag_ref[...], zero)
    diag_out[PB:, :] = jnp.where(
        both, jnp.broadcast_to(mean_ref[...], (diag_out.shape[0] - PB, PB)), zero
    )


def feature_block(points, weights, samples_twice, samples_sq):
    scaled = points * weights
    point_sq = jnp.sum(points * scaled, axis=1, keepdims=True)
    high, low = split_two(scaled)
    cross_term = dot(jnp.concatenate([high, low], axis=1), samples_twice, NT)
    return jnp.exp(cross_term - 0.5 * (point_sq + samples_sq))


def eliminate_super(x_ref, base):
    sub_ids = lax.broadcasted_iota(jnp.int32, (SUB, LANES), 0)
    groups = SUPER // SUB
    per = WIDE // SUB
    size = x_ref.shape[0]
    tiles_of = size // LANES
    after = base + SUPER
    for step in range(SUPER // WIDE):
        col0 = base + step * WIDE
        first = step * per
        lane_tiles = [t for t in range(tiles_of) if (t + 1) * LANES > col0]
        lane_tiles += [tiles_of + t for t in range(tiles_of) if t * LANES < col0 + WIDE]
        column = {}
        for g in range(first, groups):
            piece = x_ref[base + g * SUB : base + (g + 1) * SUB, col0 : col0 + WIDE]
            column[g] = [jnp.broadcast_to(piece[:, k : k + 1], (SUB, LANES)) for k in range(WIDE)]
        square = {}
        for k in range(WIDE):
            for m in range(k + 1):
                source = column[first + m // SUB][k]
                square[m, k] = jnp.broadcast_to(
                    source[m % SUB : m % SUB + 1, :], (SUB, LANES)
                )
        scale = []
        below = {}
        for k in range(WIDE):
            scale.append(lax.rsqrt(square[k, k]))
            for j in range(k + 1, WIDE):
                below[j, k] = square[k, j] * scale[k]
            for m in range(k + 1, WIDE):
                for j in range(m, WIDE):
                    square[m, j] = square[m, j] - below[m, k] * below[j, k]
        factor_cols = {}
        for g in range(first, groups):
            for k in range(WIDE):
                if g - first < k // SUB:
                    continue
                value = column[g][k]
                for m in range(k):
                    value = value - factor_cols[g, m] * below[k, m]
                factor_cols[g, k] = value * scale[k]
        for t in lane_tiles:
            lanes = slice(t * LANES, (t + 1) * LANES)
            tiles = {
                g: x_ref[base + g * SUB : base + (g + 1) * SUB, lanes]
                for g in range(first, groups)
            }
            for k in range(WIDE):
                own = first + k // SUB
                at = k % SUB
                pivot_row = jnp.broadcast_to(tiles[own][at : at + 1, :], (SUB, LANES)) * scale[k]
                mine = tiles[own] - jnp.where(sub_ids > at, factor_cols[own, k], 0.0) * pivot_row
                tiles[own] = jnp.where(sub_ids == at, pivot_row, mine)
                for g in range(own + 1, groups):
                    tiles[g] = tiles[g] - factor_cols[g, k] * pivot_row
            for g in tiles:
                x_ref[base + g * SUB : base + (g + 1) * SUB, lanes] = tiles[g]
    if after < size:
        done = x_ref[base:after, after:size]
        for low, high in (
            (after // LANES * LANES, size),
            (size, size + -(-after // LANES) * LANES),
        ):
            x_ref[after:, low:high] = x_ref[after:, low:high] - dot(
                done, x_ref[base:after, low:high], TN, HIGHEST
            )


def move_kernel(
    n_rows, n_cols,
    points_ref, xs_ref, cols_ref, rows_ref, diag_ref, inducing_ref, weights_ref,
    feat_r_out, feat_c_out, feat_p_out, cols_out, rows_out, x_out, mean_out, stats_out, y_out,
    points_c, points_r, feat_r, feat_c, trace_all,
    all_x, diag_got, diag_sum, diag_col, diag_all, cols_got, cols_sum, rows_got, rows_sum, twice,
    send_sem, recv_sem, local_sem,
):
    my_row = lax.axis_index("row")
    my_col = lax.axis_index("col")
    n_of = {"row": n_rows, "col": n_cols}
    me_of = {"row": my_row, "col": my_col}
    slot = [0]

    def peer(axis, distance):
        return lax.rem(me_of[axis] + distance, n_of[axis])

    def peer_id(axis, distance):
        if axis == "row":
            return (peer(axis, distance), my_col)
        return (my_row, peer(axis, distance))

    def send_all(axis, source, target):
        copies = []
        for distance in range(1, n_of[axis]):
            copy = pltpu.make_async_remote_copy(
                src_ref=source(distance),
                dst_ref=target(distance),
                send_sem=send_sem.at[slot[0]],
                recv_sem=recv_sem.at[slot[0]],
                device_id=peer_id(axis, distance),
                device_id_type=MESH,
            )
            slot[0] += 1
            copy.start()
            copies.append(copy)
        return copies

    def arrive(copies):
        for copy in copies:
            copy.wait_recv()

    tile_rows = feat_r.shape[0]
    tile_cols = feat_c.shape[0]
    points_count = inducing_ref.shape[0]
    loads = [
        pltpu.make_async_copy(
            inducing_ref.at[pl.ds(my_col * tile_cols, tile_cols)], points_c, local_sem.at[0]
        ),
        pltpu.make_async_copy(
            inducing_ref.at[pl.ds(my_row * tile_rows, tile_rows)], points_r, local_sem.at[3]
        ),
    ]
    for load in loads:
        load.start()

    barrier = pltpu.get_barrier_semaphore()
    for axis in ("row", "col"):
        for distance in range(1, n_of[axis]):
            pl.semaphore_signal(
                barrier, inc=1, device_id=peer_id(axis, distance), device_id_type=MESH
            )
    pl.semaphore_wait(barrier, n_rows + n_cols - 2)

    batch = xs_ref.shape[0]
    all_x[my_col, my_row] = xs_ref[...]
    xs_first = send_all("row", lambda d: xs_ref, lambda d: all_x.at[my_col, my_row])

    def slices(count, ref, axis):
        return lambda d: ref.at[pl.ds(peer(axis, d) * count, count)]

    def combine(ref, got, axis, count):
        total = ref[pl.ds(me_of[axis] * count, count), :]
        for distance in range(1, n_of[axis]):
            total = total + got[distance - 1]
        return total

    diag_count = diag_sum.shape[0]
    rows_count = rows_sum.shape[0]
    cols_count = cols_sum.shape[0]
    diag_mine = pl.ds(my_row * diag_count, diag_count)
    rows_mine = pl.ds(my_row * rows_count, rows_count)
    cols_mine = pl.ds(my_col * cols_count, cols_count)
    diag_first = send_all(
        "row", slices(diag_count, diag_ref, "row"), lambda d: diag_got.at[d - 1]
    )
    arrive(xs_first)
    xs_second = send_all("col", lambda d: all_x.at[my_col], lambda d: all_x.at[my_col])
    arrive(diag_first)
    diag_sum[...] = combine(diag_ref, diag_got, "row", diag_count)
    diag_second = send_all("col", lambda d: diag_sum, lambda d: diag_col.at[d - 1])
    arrive(xs_second)

    width = inducing_ref.shape[1]
    n_batch = n_rows * n_cols * batch
    gathered = all_x[...].reshape(n_batch, all_x.shape[3])
    samples = gathered[:, :width]
    twice[:, :width] = samples
    twice[:, width:] = samples
    values_t = jnp.transpose(gathered[:, width:].astype(F32))[:SUB, :]
    y_out[...] = values_t.astype(BF16)
    power = jnp.sum(values_t[:1, :] * values_t[:1, :], keepdims=True)
    weights = weights_ref[...]
    samples_f = samples.astype(F32)
    samples_sq = dot(jnp.broadcast_to(weights, (SUB, width)), samples_f * samples_f, NT, HIGHEST)[:1, :]

    def features_of(points):
        return feature_block(points, weights, twice[...], samples_sq)

    step_rows = min(2 * PB, tile_rows, tile_cols)

    def col_step(index, total):
        rows = pl.ds(pl.multiple_of(index * step_rows, step_rows), step_rows)
        exact = features_of(points_c[rows, :])
        feat_c[rows, :] = exact.astype(BF16)
        return total + jnp.sum((exact * exact).reshape(step_rows // SUB, SUB, n_batch), axis=0)

    def row_step(index, carry):
        rows = pl.ds(pl.multiple_of(index * step_rows, step_rows), step_rows)
        feat_r[rows, :] = features_of(points_r[rows, :]).astype(BF16)
        return carry

    loads[0].wait()
    partial = lax.fori_loop(
        0, tile_cols // step_rows, col_step, jnp.zeros((SUB, n_batch), F32)
    )
    trace_all[my_col] = jnp.broadcast_to(jnp.sum(partial, keepdims=True), (SUB, LANES))
    trace_sent = send_all("col", lambda d: trace_all.at[my_col], lambda d: trace_all.at[my_col])
    arrive(diag_second)
    total = diag_sum[...]
    for distance in range(1, n_cols):
        total = total + diag_col[distance - 1]
    diag_all[diag_mine, :] = total
    diag_third = send_all("row", lambda d: diag_all.at[diag_mine], lambda d: diag_all.at[diag_mine])
    cols_first = send_all(
        "col", slices(cols_count, cols_ref, "col"), lambda d: cols_got.at[d - 1]
    )
    rows_first = send_all(
        "row", slices(rows_count, rows_ref, "row"), lambda d: rows_got.at[d - 1]
    )
    loads[1].wait()
    lax.fori_loop(0, tile_rows // step_rows, row_step, 0)
    stores = [
        pltpu.make_async_copy(feat_r, feat_r_out, local_sem.at[1]),
        pltpu.make_async_copy(feat_c, feat_c_out, local_sem.at[2]),
    ]
    for store in stores:
        store.start()
    feat_p = features_of(points_ref[...]).astype(BF16)
    feat_p_out[...] = feat_p
    gram_p = dot(feat_p, feat_p, NT)
    arrive(trace_sent)
    trace_sum = trace_all[0]
    for col in range(1, n_cols):
        trace_sum = trace_sum + trace_all[col]
    trace_scale = trace_sum[:1, :1] / points_count
    gram_scale = RATE / trace_scale
    mean_scale = RATE * lax.rsqrt(trace_scale * (power / n_batch + EPSILON))
    stats_out[0:1, :] = jnp.broadcast_to(gram_scale, (1, LANES))
    stats_out[1:2, :] = jnp.broadcast_to(mean_scale, (1, LANES))
    stats_out[2:, :] = jnp.zeros((SUB - 2, LANES), F32)

    arrive(diag_third)
    mean_out[...] = diag_all[PB : PB + SUB, :]
    x_out[:, :PB] = (1.0 - RATE) * diag_all[:PB, :] + gram_scale * gram_p
    x_out[:, PB:] = jnp.where(
        lax.broadcasted_iota(jnp.int32, (PB, PB), 0) == lax.broadcasted_iota(jnp.int32, (PB, PB), 1),
        1.0,
        0.0,
    )
    for base in range(0, PB, SUPER):
        eliminate_super(x_out, base)
        if base == 0:
            arrive(cols_first)
            cols_sum[...] = combine(cols_ref, cols_got, "col", cols_count)
            cols_out[cols_mine, :] = cols_sum[...]
            cols_second = send_all("col", lambda d: cols_sum, lambda d: cols_out.at[cols_mine])
            arrive(rows_first)
            rows_sum[...] = combine(rows_ref, rows_got, "row", rows_count)
            rows_out[rows_mine, :] = rows_sum[...]
            rows_second = send_all("row", lambda d: rows_sum, lambda d: rows_out.at[rows_mine])
    arrive(rows_second)
    arrive(cols_second)
    for copies in (
        xs_first, xs_second, trace_sent, diag_first, diag_second, diag_third,
        rows_first, rows_second, cols_first, cols_second,
    ):
        for copy in copies:
            copy.wait_send()
    for store in stores:
        store.wait()


def tile_kernel(
    info,
    prec_ref, feat_r_ref, feat_c_ref, feat_p_ref, cols_ref, rows_ref, x_ref, mean_p_ref,
    stats_ref, y_ref, mean_ref,
    out_ref, mean_out,
    solved, solved_parts, inverse_high, inverse_low, head,
):
    step = pl.program_id(0)
    in_row = info[2] == 1
    in_col = info[3] == 1
    keep = 1.0 - RATE
    gram_scale = stats_ref[0:1, 0:1]
    mean_scale = stats_ref[1:2, 0:1]

    @pl.when(step == 0)
    def _():
        inverse = x_ref[:, PB:]
        high, low = split_two(inverse)
        inverse_high[...] = high
        inverse_low[...] = low
        joined = keep * rows_ref[...].astype(F32) + gram_scale * dot(feat_p_ref[...], feat_c_ref[...], NT)
        result = dot_split((high, low), split_two(joined), NN)
        solved[...] = result
        result_high, result_low = split_two(result)
        solved_parts[:PB, :] = result_high
        solved_parts[PB : 2 * PB, :] = result_high
        solved_parts[2 * PB :, :] = result_low
        fit = dot(y_ref[...], feat_p_ref[...], NT)
        head[...] = dot(keep * mean_p_ref[...] + mean_scale * fit, inverse, NT, HIGHEST)

    feat_r = feat_r_ref[...]
    piece = keep * cols_ref[...].astype(F32) + gram_scale * dot(feat_r, feat_p_ref[...], NT)
    wide = dot_split(split_two(piece), (inverse_high[...], inverse_low[...]), NT)
    wide_high, wide_low = split_two(wide)
    wide_parts = jnp.concatenate([wide_high, wide_low, wide_high], axis=1)
    for low in range(0, prec_ref.shape[1], CHUNK):
        lanes = slice(low, low + CHUNK)
        gram = dot(feat_r, feat_c_ref[lanes, :], NT)
        out_ref[:, lanes] = (keep * prec_ref[:, lanes] + gram_scale * gram) - dot(
            wide_parts, solved_parts[:, lanes], NN
        )
    fit = dot(y_ref[...], feat_r, NT)
    mean_next = (
        keep * mean_ref[...] + mean_scale * fit[:1, :] - dot_split(split_two(head[...]), (wide_high, wide_low), NT)[:1, :]
    )
    mean_out[...] = mean_next
    col0 = pl.multiple_of(info[1] * PB, PB)

    @pl.when(in_col)
    def _():
        out_ref[:, pl.ds(col0, PB)] = wide

    here = jnp.logical_and(in_row, step == info[0])

    @pl.when(here)
    def _():
        out_ref[...] = solved[...]
        mean_out[...] = head[:1, :]

    @pl.when(jnp.logical_and(here, in_col))
    def _():
        factor = jnp.transpose(x_ref[:, :PB])
        lower = lax.broadcasted_iota(jnp.int32, (PB, PB), 0) >= lax.broadcasted_iota(
            jnp.int32, (PB, PB), 1
        )
        out_ref[:, pl.ds(col0, PB)] = jnp.where(lower, factor, 0.0)


def whole(memory=pltpu.VMEM):
    return pl.BlockSpec(memory_space=memory)


def local(pool, targets, picks, inducing, inv_sq_lengths, prec_old, mean_old, panel):
    n_rows = lax.axis_size("row")
    n_cols = lax.axis_size("col")
    my_row = lax.axis_index("row")
    my_col = lax.axis_index("col")
    tile_rows, tile_cols = prec_old.shape
    batch = picks.shape[0]
    n_batch = batch * n_rows * n_cols
    width = pool.shape[1]
    row_blocks = tile_rows // PB
    col_blocks = tile_cols // PB
    index = panel[0]
    info = jnp.stack(
        [
            lax.rem(index, row_blocks),
            lax.rem(index, col_blocks),
            (index // row_blocks == my_row).astype(jnp.int32),
            (index // col_blocks == my_col).astype(jnp.int32),
            index,
        ]
    )
    mean_row = mean_old.reshape(1, tile_rows)
    shape = jax.ShapeDtypeStruct
    diag_count = -(-(PB + SUB) // (n_rows * SUB)) * SUB
    diag_rows = diag_count * n_rows
    full = lambda *dims: pl.BlockSpec(dims, lambda i, info: (0,) * len(dims))
    xs, cols, rows, diag, points = pl.pallas_call(
        prep_kernel,
        grid_spec=pltpu.PrefetchScalarGridSpec(
            num_scalar_prefetch=1,
            grid=(1,),
            in_specs=[
                full(1, batch),
                full(*pool.shape),
                full(1, pool.shape[0]),
                pl.BlockSpec((tile_rows, PB), lambda i, info: (0, info[1])),
                pl.BlockSpec((PB, tile_cols), lambda i, info: (info[0], 0)),
                pl.BlockSpec((PB, PB), lambda i, info: (info[0], info[1])),
                pl.BlockSpec((1, PB), lambda i, info: (0, info[0])),
                pl.BlockSpec((PB, width), lambda i, info: (info[4], 0)),
            ],
            out_specs=[
                full(batch, width + LANES),
                full(tile_rows, PB),
                full(PB, tile_cols),
                full(diag_rows, PB),
                full(PB, width),
            ],
        ),
        out_shape=[
            shape((batch, width + LANES), BF16),
            shape((tile_rows, PB), BF16),
            shape((PB, tile_cols), BF16),
            shape((diag_rows, PB), F32),
            shape((PB, width), F32),
        ],
        compiler_params=pltpu.CompilerParams(vmem_limit_bytes=VMEM),
        name="prep",
    )(
        info, picks.reshape(1, batch), pool, targets.reshape(1, -1),
        prec_old, prec_old, prec_old, mean_row, inducing,
    )
    sems = 5 * (n_rows - 1) + 5 * (n_cols - 1)
    cols_count = tile_rows // n_cols
    rows_count = PB // n_rows
    moved = pl.pallas_call(
        functools.partial(move_kernel, n_rows, n_cols),
        in_specs=[whole()] * 5 + [whole(pl.ANY), whole()],
        out_specs=[whole(pl.ANY)] * 2 + [whole()] * 7,
        out_shape=[
            shape((tile_rows, n_batch), BF16),
            shape((tile_cols, n_batch), BF16),
            shape((PB, n_batch), BF16),
            shape((tile_rows, PB), BF16),
            shape((PB, tile_cols), BF16),
            shape((PB, 2 * PB), F32),
            shape((SUB, PB), F32),
            shape((SUB, LANES), F32),
            shape((SUB, n_batch), BF16),
        ],
        scratch_shapes=[
            pltpu.VMEM((tile_cols, width), F32),
            pltpu.VMEM((tile_rows, width), F32),
            pltpu.VMEM((tile_rows, n_batch), BF16),
            pltpu.VMEM((tile_cols, n_batch), BF16),
            pltpu.VMEM((n_cols, SUB, LANES), F32),
            pltpu.VMEM((n_cols, n_rows, batch, width + LANES), BF16),
            pltpu.VMEM((n_rows - 1, diag_count, PB), F32),
            pltpu.VMEM((diag_count, PB), F32),
            pltpu.VMEM((n_cols - 1, diag_count, PB), F32),
            pltpu.VMEM((diag_rows, PB), F32),
            pltpu.VMEM((n_cols - 1, cols_count, PB), BF16),
            pltpu.VMEM((cols_count, PB), BF16),
            pltpu.VMEM((n_rows - 1, rows_count, tile_cols), BF16),
            pltpu.VMEM((rows_count, tile_cols), BF16),
            pltpu.VMEM((n_batch, 2 * width), BF16),
            pltpu.SemaphoreType.DMA((sems,)),
            pltpu.SemaphoreType.DMA((sems,)),
            pltpu.SemaphoreType.DMA((4,)),
        ],
        compiler_params=pltpu.CompilerParams(
            collective_id=0, has_side_effects=True, vmem_limit_bytes=VMEM
        ),
        name="move",
    )(points, xs, cols, rows, diag, inducing, inv_sq_lengths.reshape(1, width))
    feat_r, feat_c, feat_p, got_cols, got_rows, x, mean_p, stats, y = moved
    step_rows = PB
    updated, mean_next = pl.pallas_call(
        tile_kernel,
        grid_spec=pltpu.PrefetchScalarGridSpec(
            num_scalar_prefetch=1,
            grid=(tile_rows // step_rows,),
            in_specs=[
                pl.BlockSpec((step_rows, tile_cols), lambda i, info: (i, 0)),
                pl.BlockSpec((step_rows, n_batch), lambda i, info: (i, 0)),
                full(tile_cols, n_batch),
                full(PB, n_batch),
                pl.BlockSpec((step_rows, PB), lambda i, info: (i, 0)),
                full(PB, tile_cols),
                full(PB, 2 * PB),
                full(SUB, PB),
                full(SUB, LANES),
                full(SUB, n_batch),
                pl.BlockSpec((1, step_rows), lambda i, info: (0, i)),
            ],
            out_specs=[
                pl.BlockSpec((step_rows, tile_cols), lambda i, info: (i, 0)),
                pl.BlockSpec((1, step_rows), lambda i, info: (0, i)),
            ],
            scratch_shapes=[
                pltpu.VMEM((PB, tile_cols), F32),
                pltpu.VMEM((3 * PB, tile_cols), BF16),
                pltpu.VMEM((PB, PB), BF16),
                pltpu.VMEM((PB, PB), BF16),
                pltpu.VMEM((SUB, PB), F32),
            ],
        ),
        out_shape=[shape((tile_rows, tile_cols), F32), shape((1, tile_rows), F32)],
        compiler_params=pltpu.CompilerParams(vmem_limit_bytes=VMEM),
        name="tile",
    )(
        info, prec_old, feat_r, feat_c, feat_p, got_cols, got_rows, x, mean_p, stats, y, mean_row,
    )
    return updated, mean_next.reshape(tile_rows)


def solution(mesh):
    in_specs = (
        P(("row", "col"), None),
        P(("row", "col")),
        P(("row", "col")),
        P(),
        P(),
        P("row", "col"),
        P("row"),
        P(),
    )
    out_specs = (P("row", "col"), P("row"))
    return jax.shard_map(local, mesh=mesh, in_specs=in_specs, out_specs=out_specs, check_vma=False)
```
